128 devices in a mesh: band: 32 (over x, z, core), sub: 4 (over y).
Axes of the slice: x: 4, y: 4, z: 4, core: 2. Of those that a mesh axis runs over, the one named last changes fastest.
Arguments:
- grid_input: bfloat16 [262144, 227], P(('band', 'sub')), may hold values from -6 to 6
- grid_send: int32 [384, 4, 128], P(('band', 'sub')), may hold values from 0 to 2047, as said below
- grid_edge_src: int32 [1048576], P(('band', 'sub')), may hold values from 0 to 1535, as said below
- grid_edge_dst: int32 [1048576], P(('band', 'sub')), may hold values from 0 to 319
- edge_count: int32 [128], P(('band', 'sub')), may hold values from 1536 to 8192, as said below
- grid_edge_geo: bfloat16 [4, 1048576], P(None, ('band', 'sub')), may hold values from -6 to 6
- mesh_embed: bfloat16 [40960, 512], P(('band', 'sub')), may hold values from -6 to 6
- mesh_near_send: int32 [384, 4, 64], P(('band', 'sub')), may hold values from 0 to 319, as said below
- mesh_far_send: int32 [16384, 2], P(('band', 'sub')), may hold values from 0 to 319, as said below
- mesh_edge_src: int32 [327680], P(('band', 'sub')), may hold values from 0 to 1343, as said below
- mesh_edge_dst: int32 [327680], P(('band', 'sub')), may hold values from 0 to 319
- mesh_edge_lat: bfloat16 [327680, 512], P(('band', 'sub')), may hold values from -6 to 6
- enc_in: bfloat16 [227, 512], replicated, may hold values from -0.375 to 0.375
- enc_out: bfloat16 [512, 512], replicated, may hold values from -0.25 to 0.25
- send_proj: bfloat16 [512, 512], replicated, may hold values from -0.25 to 0.25
- recv_proj: bfloat16 [512, 512], replicated, may hold values from -0.25 to 0.25
- geo_proj: bfloat16 [4, 512], replicated, may hold values from -3 to 3
- msg_weight: bfloat16 [512, 512], replicated, may hold values from -0.25 to 0.25
- node_self: bfloat16 [512, 512], replicated, may hold values from -0.25 to 0.25
- node_agg: bfloat16 [512, 512], replicated, may hold values from -0.25 to 0.25
- node_out: bfloat16 [512, 512], replicated, may hold values from -0.25 to 0.25
- mesh_gain: float32 [512], replicated, may hold values from 0.1 to 1.9
- proc_send: bfloat16 [512, 512], replicated, may hold values from -0.25 to 0.25
- proc_recv: bfloat16 [512, 512], replicated, may hold values from -0.25 to 0.25
- edge_self: bfloat16 [512, 512], replicated, may hold values from -0.25 to 0.25
- edge_out: bfloat16 [512, 512], replicated, may hold values from -0.25 to 0.25
- upd_self: bfloat16 [512, 512], replicated, may hold values from -0.25 to 0.25
- upd_agg: bfloat16 [512, 512], replicated, may hold values from -0.25 to 0.25
- upd_out: bfloat16 [512, 512], replicated, may hold values from -0.25 to 0.25
- out_gain: float32 [512], replicated, may hold values from 0.1 to 1.9
Outputs:
- mesh_out: bfloat16 [40960, 512], P(('band', 'sub'))
The draws below stay inside these ranges and needn't reach their ends.
Inputs may be any that keep to these rules, and one draw needn't show every extreme that they name: `grid_send`: local grid rows of the sending device. `grid_edge_src`: on each device the first edges use every received position whose source band exists exactly once, in order of position; later edges use such positions at random; positions from a band outside the grid are never used. `edge_count`: devices of the first and last band have 8192 live edges; every other device has at least 3 * 128 times the number of sub devices. `mesh_near_send`: local mesh rows of the sending device. `mesh_far_send`: local mesh rows of the sending device. `mesh_edge_src`: positions below 320 are the device's own rows; every received row from an existing band and every far row is used by exactly one edge of its device; rows from a band outside the grid are never used.
All inputs are finite; a program needn't handle non-finite values.
Results may differ from the reference program's by a relative error of at most 0.015.
Values may be sent and summed in bfloat16 or wider, within the bound.
No kernel may reach another device: no remote copies, remote signals or barrier semaphores. Data moves between devices by JAX's collectives and lax.ppermute only.
A program may use at most 64 MiB of HBM per device.

```python
import jax
import jax.numpy as jnp
from jax import lax

D_IN = 227
LAT = 512
G_DEV = 2048
E_DEV = 8192
CAP = 128
M_DEV = 320
NCAP = 64
FCAP = 2
ME_DEV = 2560
GRID = 262144
GEDGES = 1048576
MESH = 40960
MEDGES = 327680
N_BAND = 32
N_SUB = 4


def live_counts(key):
    count_key = jax.random.fold_in(key, 5)
    devices = N_BAND * N_SUB
    band_index = jnp.arange(devices, dtype=jnp.int32) // N_SUB
    polar_rows = (band_index == 0) | (band_index == N_BAND - 1)
    extra_live = jax.random.randint(count_key, (devices,), 0, (E_DEV - 3 * N_SUB * CAP) // 2 + 1, dtype=jnp.int32)
    extra_live = extra_live.at[N_SUB].set(0)
    return jnp.where(polar_rows, E_DEV, 3 * N_SUB * CAP + extra_live).astype(jnp.int32)


def draw_edge_count(key, part):
    return live_counts(key)


def valid_order(slot_cap):
    devices = N_BAND * N_SUB
    slot_total = 3 * N_SUB * slot_cap
    band_index = jnp.arange(devices, dtype=jnp.int32) // N_SUB
    slots = jnp.arange(slot_total, dtype=jnp.int32)
    offsets = slots // (N_SUB * slot_cap)
    source_band = band_index[:, None] - offsets[None, :] + 1
    invalid = ((source_band < 0) | (source_band >= N_BAND)).astype(jnp.int32)
    scores = invalid * slot_total + slots[None, :]
    ordered = jnp.argsort(scores, axis=1, stable=True).astype(jnp.int32)
    valid_total = slot_total - jnp.sum(invalid, axis=1).astype(jnp.int32)
    return (ordered, valid_total)


def draw_grid_send(key, part):
    key = jax.random.fold_in(key, 11)
    devices = N_BAND * N_SUB
    picks = jax.random.randint(key, (devices, 3 * N_SUB * CAP), 0, G_DEV, dtype=jnp.int32)
    picks = picks.at[:, 0].set(0).at[:, -1].set(G_DEV - 1)
    return picks.reshape(devices * 3, N_SUB, CAP).astype(jnp.int32)


def draw_grid_edge_src(key, part):
    key = jax.random.fold_in(key, 13)
    devices = N_BAND * N_SUB
    slot_total = 3 * N_SUB * CAP
    ordered, valid_total = valid_order(CAP)
    positions = jnp.arange(E_DEV, dtype=jnp.int32)
    chosen = jax.random.randint(key, (devices, E_DEV), 0, valid_total[:, None], dtype=jnp.int32)
    pointer = jnp.where(positions[None, :] < valid_total[:, None], jnp.minimum(positions[None, :], slot_total - 1), chosen)
    result = jnp.take_along_axis(ordered, pointer, axis=1)
    return result.reshape(devices * E_DEV).astype(jnp.int32)


def draw_grid_edge_dst(key, part):
    key = jax.random.fold_in(key, 17)
    devices = N_BAND * N_SUB
    targets = jax.random.randint(key, (devices, E_DEV), 0, M_DEV, dtype=jnp.int32)
    targets = targets.at[:, 0].set(0).at[:, 1].set(M_DEV - 1)
    return targets.reshape(devices * E_DEV).astype(jnp.int32)


def draw_mesh_near_send(key, part):
    key = jax.random.fold_in(key, 19)
    devices = N_BAND * N_SUB
    picks = jax.random.randint(key, (devices, 3 * N_SUB * NCAP), 0, M_DEV, dtype=jnp.int32)
    picks = picks.at[:, 0].set(0).at[:, -1].set(M_DEV - 1)
    return picks.reshape(devices * 3, N_SUB, NCAP).astype(jnp.int32)


def draw_mesh_far_send(key, part):
    key = jax.random.fold_in(key, 31)
    devices = N_BAND * N_SUB
    picks = jax.random.randint(key, (devices, devices * FCAP), 0, M_DEV, dtype=jnp.int32)
    picks = picks.at[:, 0].set(0).at[:, -1].set(M_DEV - 1)
    return picks.reshape(devices * devices, FCAP).astype(jnp.int32)


def draw_mesh_edge_src(key, part):
    key = jax.random.fold_in(key, 23)
    devices = N_BAND * N_SUB
    near_total = 3 * N_SUB * NCAP
    far_total = devices * FCAP
    local_key, perm_key = jax.random.split(key)
    ordered, valid_near = valid_order(NCAP)
    positions = jnp.arange(ME_DEV, dtype=jnp.int32)
    local_rows = jax.random.randint(local_key, (devices, ME_DEV), 0, M_DEV, dtype=jnp.int32)
    local_rows = local_rows.at[:, near_total + far_total].set(0).at[:, near_total + far_total + 1].set(M_DEV - 1)
    near_pick = jnp.take_along_axis(ordered, jnp.minimum(positions[None, :], near_total - 1) + jnp.zeros((devices, 1), jnp.int32), axis=1)
    near_rows = M_DEV + near_pick
    far_rows = M_DEV + near_total + positions[None, :] - valid_near[:, None]
    in_near = positions[None, :] < valid_near[:, None]
    in_far = (positions[None, :] >= valid_near[:, None]) & (positions[None, :] < valid_near[:, None] + far_total)
    sources = jnp.where(in_near, near_rows, jnp.where(in_far, far_rows, local_rows))
    orders = jax.vmap(lambda sub_key: jax.random.permutation(sub_key, ME_DEV))(jax.random.split(perm_key, devices))
    sources = jnp.take_along_axis(sources, orders.astype(jnp.int32), axis=1)
    return sources.reshape(devices * ME_DEV).astype(jnp.int32)


def draw_mesh_edge_dst(key, part):
    key = jax.random.fold_in(key, 29)
    devices = N_BAND * N_SUB
    targets = jax.random.randint(key, (devices, ME_DEV), 0, M_DEV, dtype=jnp.int32)
    targets = targets.at[:, 0].set(0).at[:, 1].set(M_DEV - 1)
    return targets.reshape(devices * ME_DEV).astype(jnp.int32)


def block_levels(own_key, shape, cuts, low, largest):
    gain = 1.0
    for dim, blocks in cuts:
        draws = jax.random.uniform(jax.random.fold_in(jax.random.fold_in(own_key, 6), dim), (blocks,), jnp.float32, low / len(cuts), largest / len(cuts))
        gain = gain * jnp.repeat(jnp.exp(draws), shape[dim] // blocks).reshape((-1,) + (1,) * (len(shape) - 1 - dim))
    return gain


def scatter_about(own_key, extent, deviation, limit, cuts=(), kind=jnp.bfloat16):
    array = deviation * jax.random.normal(own_key, extent, jnp.float32)
    if cuts:
        array = array * block_levels(own_key, extent, cuts, -0.22, 0.18)
    return jnp.clip(array, -limit, limit).astype(kind)


def setup_inputs(seed: int = 0) -> dict:
    keys = jax.random.split(jax.random.key(seed), 31)
    return {
        "grid_input": scatter_about(keys[0], (GRID, D_IN), 1.0, 6.0, ((0, 128),)),
        "grid_send": draw_grid_send(jax.random.fold_in(keys[30], 71), 0),
        "grid_edge_src": draw_grid_edge_src(jax.random.fold_in(keys[30], 71), 0),
        "grid_edge_dst": draw_grid_edge_dst(jax.random.fold_in(keys[30], 71), 0),
        "edge_count": draw_edge_count(jax.random.fold_in(keys[30], 71), 0),
        "grid_edge_geo": scatter_about(keys[5], (4, GEDGES), 1.0, 6.0, ((1, 128),)),
        "mesh_embed": scatter_about(keys[6], (MESH, LAT), 1.0, 6.0, ((0, 128),)),
        "mesh_near_send": draw_mesh_near_send(jax.random.fold_in(keys[30], 71), 0),
        "mesh_far_send": draw_mesh_far_send(jax.random.fold_in(keys[30], 71), 0),
        "mesh_edge_src": draw_mesh_edge_src(jax.random.fold_in(keys[30], 71), 0),
        "mesh_edge_dst": draw_mesh_edge_dst(jax.random.fold_in(keys[30], 71), 0),
        "mesh_edge_lat": scatter_about(keys[11], (MEDGES, LAT), 1.0, 6.0, ((0, 128),)),
        "enc_in": scatter_about(keys[12], (D_IN, LAT), D_IN ** -0.5, 0.375),
        "enc_out": scatter_about(keys[13], (LAT, LAT), LAT ** -0.5, 0.25),
        "send_proj": scatter_about(keys[14], (LAT, LAT), LAT ** -0.5, 0.25),
        "recv_proj": scatter_about(keys[15], (LAT, LAT), LAT ** -0.5, 0.25),
        "geo_proj": scatter_about(keys[16], (4, LAT), 4 ** -0.5, 3.0),
        "msg_weight": scatter_about(keys[17], (LAT, LAT), LAT ** -0.5, 0.25),
        "node_self": scatter_about(keys[18], (LAT, LAT), LAT ** -0.5, 0.25),
        "node_agg": scatter_about(keys[19], (LAT, LAT), LAT ** -0.5, 0.25),
        "node_out": scatter_about(keys[20], (LAT, LAT), LAT ** -0.5, 0.25),
        "mesh_gain": jnp.clip(1.0 + 0.18 * jax.random.normal(keys[21], (LAT,), jnp.float32), 0.1, 1.9),
        "proc_send": scatter_about(keys[22], (LAT, LAT), LAT ** -0.5, 0.25),
        "proc_recv": scatter_about(keys[23], (LAT, LAT), LAT ** -0.5, 0.25),
        "edge_self": scatter_about(keys[24], (LAT, LAT), LAT ** -0.5, 0.25),
        "edge_out": scatter_about(keys[25], (LAT, LAT), LAT ** -0.5, 0.25),
        "upd_self": scatter_about(keys[26], (LAT, LAT), LAT ** -0.5, 0.25),
        "upd_agg": scatter_about(keys[27], (LAT, LAT), LAT ** -0.5, 0.25),
        "upd_out": scatter_about(keys[28], (LAT, LAT), LAT ** -0.5, 0.25),
        "out_gain": jnp.clip(1.0 + 0.18 * jax.random.normal(keys[29], (LAT,), jnp.float32), 0.1, 1.9),
    }


def layer_norm(values):
    row_mean = lax.optimization_barrier(jnp.mean(values, axis=-1, keepdims=True))
    centred = values - row_mean
    variance = lax.optimization_barrier(jnp.mean(centred * centred, axis=-1, keepdims=True))
    return centred * lax.rsqrt(variance + 1e-05)

def project(inputs, weight):
    return jnp.dot(inputs, weight, preferred_element_type=jnp.float32).astype(jnp.bfloat16)

def encode_rows(inputs, enc_in, enc_out):
    hidden = jax.nn.silu(jnp.dot(inputs, enc_in, preferred_element_type=jnp.float32)).astype(jnp.bfloat16)
    return layer_norm(jnp.dot(hidden, enc_out, preferred_element_type=jnp.float32)).astype(jnp.bfloat16)

def geometry_term(geometry, geo_proj):
    return lax.dot_general(geometry, geo_proj, (((0,), (0,)), ((), ())), preferred_element_type=jnp.float32)

def band_rows(table, sends, device, band_count, sub_count, width):
    take_rows = jax.vmap(lambda table_rows, picks: jnp.take(table_rows, picks, axis=0))
    band_index = device // sub_count
    sub_index = device % sub_count
    blocks = []
    for offset in range(3):
        source_band = band_index - offset + 1
        inside = (source_band >= 0) & (source_band < band_count)
        clipped = jnp.clip(source_band, 0, band_count - 1)
        picks = sends[clipped, :, offset, sub_index, :]
        picked = take_rows(table[clipped], picks)
        blocks.append(jnp.where(inside, picked, jnp.zeros_like(picked)))
    return jnp.stack(blocks).reshape(-1, width)

def reference(grid_input, grid_send, grid_edge_src, grid_edge_dst, edge_count, grid_edge_geo, mesh_embed, mesh_near_send, mesh_far_send, mesh_edge_src, mesh_edge_dst, mesh_edge_lat, enc_in, enc_out, send_proj, recv_proj, geo_proj, msg_weight, node_self, node_agg, node_out, mesh_gain, proc_send, proc_recv, edge_self, edge_out, upd_self, upd_agg, upd_out, out_gain):
    band_count = N_BAND
    sub_count = N_SUB
    devices = band_count * sub_count
    grid = grid_input.reshape(devices, G_DEV, D_IN)
    sender = lax.map(lambda grid_rows: project(encode_rows(grid_rows, enc_in, enc_out), send_proj), grid)
    sender = sender.reshape(band_count, sub_count, G_DEV, LAT)
    sends = grid_send.reshape(band_count, sub_count, 3, sub_count, CAP)
    sources = grid_edge_src.reshape(devices, E_DEV)
    targets = grid_edge_dst.reshape(devices, E_DEV)
    geometry = jnp.transpose(grid_edge_geo.reshape(4, devices, E_DEV), (1, 0, 2))
    embeds = mesh_embed.reshape(devices, M_DEV, LAT)
    take_rows = jax.vmap(lambda table_rows, picks: jnp.take(table_rows, picks, axis=0))

    def encode_mesh(device):
        lookup = band_rows(sender, sends, device, band_count, sub_count, LAT)
        own_embed = embeds[device]
        receiver = project(own_embed, recv_proj)
        edge_targets = targets[device]
        pre_act = lookup[sources[device]].astype(jnp.float32) + receiver[edge_targets].astype(jnp.float32) + geometry_term(geometry[device], geo_proj)
        edge_act = jax.nn.silu(pre_act).astype(jnp.bfloat16)
        live_mask = jnp.arange(E_DEV, dtype=jnp.int32) < edge_count[device]
        message = jnp.where(live_mask[:, None], jnp.dot(edge_act, msg_weight, preferred_element_type=jnp.float32), jnp.zeros((), jnp.float32)).astype(jnp.bfloat16)
        inflow = jax.ops.segment_sum(message.astype(jnp.float32), edge_targets, num_segments=M_DEV).astype(jnp.bfloat16)
        node_act = jax.nn.silu(jnp.dot(own_embed, node_self, preferred_element_type=jnp.float32) + jnp.dot(inflow, node_agg, preferred_element_type=jnp.float32)).astype(jnp.bfloat16)
        branch = layer_norm(jnp.dot(node_act, node_out, preferred_element_type=jnp.float32)) * mesh_gain
        return (own_embed.astype(jnp.float32) + branch).astype(jnp.bfloat16)
    device_ids = jnp.arange(devices, dtype=jnp.int32)
    mesh_latent = lax.map(encode_mesh, device_ids)
    mesh_sender = lax.map(lambda latent: project(latent, proc_send), mesh_latent)
    sender_bands = mesh_sender.reshape(band_count, sub_count, M_DEV, LAT)
    near_sends = mesh_near_send.reshape(band_count, sub_count, 3, sub_count, NCAP)
    far_sends = mesh_far_send.reshape(devices, devices, FCAP)
    edge_sources = mesh_edge_src.reshape(devices, ME_DEV)
    edge_dests = mesh_edge_dst.reshape(devices, ME_DEV)
    edge_lats = mesh_edge_lat.reshape(devices, ME_DEV, LAT)

    def process(device):
        near_rows = band_rows(sender_bands, near_sends, device, band_count, sub_count, LAT)
        far_rows = take_rows(mesh_sender, far_sends[:, device, :]).reshape(devices * FCAP, LAT)
        lookup = jnp.concatenate([mesh_sender[device], near_rows, far_rows], axis=0)
        own_latent = mesh_latent[device]
        target_rows = project(own_latent, proc_recv)
        dests = edge_dests[device]
        lats = edge_lats[device]
        edge_pre = jnp.dot(lats, edge_self, preferred_element_type=jnp.float32) + lookup[edge_sources[device]].astype(jnp.float32) + target_rows[dests].astype(jnp.float32)
        edge_hidden = jax.nn.silu(edge_pre).astype(jnp.bfloat16)
        edge_new = (lats.astype(jnp.float32) + layer_norm(jnp.dot(edge_hidden, edge_out, preferred_element_type=jnp.float32))).astype(jnp.bfloat16)
        inflow = jax.ops.segment_sum(edge_new.astype(jnp.float32), dests, num_segments=M_DEV).astype(jnp.bfloat16)
        upd_act = jax.nn.silu(jnp.dot(own_latent, upd_self, preferred_element_type=jnp.float32) + jnp.dot(inflow, upd_agg, preferred_element_type=jnp.float32)).astype(jnp.bfloat16)
        branch = layer_norm(jnp.dot(upd_act, upd_out, preferred_element_type=jnp.float32)) * out_gain
        return (own_latent.astype(jnp.float32) + branch).astype(jnp.bfloat16)
    return lax.map(process, device_ids).reshape(devices * M_DEV, LAT)
```

```python
import functools

import jax
import jax.numpy as jnp
from jax import lax
from jax.experimental import pallas as pl
from jax.experimental.pallas import tpu as pltpu
from jax.sharding import PartitionSpec as P

LANES = 128
EDGE_BLOCK = 512
VMEM_BYTES = 48 * 1024 * 1024


def shifted(value, steps):
    count = lax.axis_size("band")
    first, last = (max(0, -steps), min(count, count - steps))
    return lax.ppermute(value, "band", [(source, source + steps) for source in range(first, last)])


def layer_norm(values):
    row_mean = jnp.mean(values, axis=-1, keepdims=True)
    centred = values - row_mean
    variance = jnp.mean(centred * centred, axis=-1, keepdims=True)
    return centred * lax.rsqrt(variance + 1e-05)


def silu(values):
    half = 0.5 * values
    return half + half * jnp.tanh(half)


def dot(left, right):
    return jnp.dot(left, right, preferred_element_type=jnp.float32)


def half(values):
    return values.astype(jnp.bfloat16)


def column(row):
    return jnp.broadcast_to(row, (LANES, LANES)).T


def columns(ref, first, count):
    return jnp.concatenate([column(ref[pl.ds(first + k, 1), :]) for k in range(count)], axis=0)


def row_of(ref, first, count):
    return jnp.concatenate([ref[pl.ds(first + k, 1), :] for k in range(count)], axis=1)


def picks(indices, width, offset=0):
    lane = lax.broadcasted_iota(jnp.int32, indices.shape, 1)
    parts = [
        half(jnp.where(indices == lane + (offset + first), 1.0, 0.0))
        for first in range(0, width, LANES)
    ]
    return jnp.concatenate(parts, axis=1)


def scatter_picks(row, height):
    shape = (height, row.shape[1])
    sub = lax.broadcasted_iota(jnp.int32, shape, 0)
    return half(jnp.where(sub == jnp.broadcast_to(row, shape), 1.0, 0.0))


def whole(*shape):
    return pl.BlockSpec(memory_space=pltpu.VMEM)


def in_smem():
    return pl.BlockSpec(memory_space=pltpu.SMEM)


def local_call(kernel, out_shape, in_specs, scratch=(), flops=0, nbytes=0):
    return pl.pallas_call(
        kernel,
        out_shape=out_shape,
        in_specs=in_specs,
        out_specs=jax.tree.map(lambda _: pl.BlockSpec(memory_space=pltpu.VMEM), out_shape),
        scratch_shapes=list(scratch),
        compiler_params=pltpu.CompilerParams(vmem_limit_bytes=VMEM_BYTES),
        cost_estimate=pl.CostEstimate(flops=flops, bytes_accessed=nbytes, transcendentals=0),
    )


def pick_grid_kernel(send_ref, grid_ref, out_ref):
    rows, width = grid_ref.shape
    slots = send_ref.shape[0]
    out_ref[...] = jnp.zeros_like(out_ref)

    def step(k, carry):
        onehot = picks(columns(send_ref, 2 * k, 2), rows)
        out_ref[pl.ds(pl.multiple_of(2 * k * LANES, 2 * LANES), 2 * LANES), 0:width] = half(
            dot(onehot, grid_ref[...])
        )
        return carry

    lax.fori_loop(0, slots // 2, step, 0)


def encoder_kernel(
    place_ref,
    live_ref,
    first_ref,
    second_ref,
    third_ref,
    src_ref,
    dst_ref,
    geo_ref,
    embed_ref,
    near_ref,
    far_ref,
    enc_in_ref,
    enc_out_ref,
    send_proj_ref,
    recv_proj_ref,
    geo_proj_ref,
    msg_ref,
    node_self_ref,
    node_agg_ref,
    node_out_ref,
    gain_ref,
    proc_send_ref,
    proc_recv_ref,
    latent_ref,
    pair_ref,
    out_ref,
    table_ref,
    enc_ref,
    sum_ref,
):
    mesh_rows, latent = embed_ref.shape
    chunk = first_ref.shape[0]
    base = table_ref.shape[0] - 3 * chunk
    geo_rows = geo_ref.shape[0]
    is_first = place_ref[0] == 0
    is_last = place_ref[0] == place_ref[1] - 1
    polar = is_first | is_last
    live = live_ref[0]

    enc_ref[...] = jnp.zeros_like(enc_ref)
    enc_ref[0 : enc_in_ref.shape[0], :] = enc_in_ref[...]
    table_ref[0:mesh_rows, :] = half(dot(embed_ref[...], recv_proj_ref[...]))
    table_ref[mesh_rows:base, :] = jnp.concatenate(
        [
            geo_proj_ref[...].astype(jnp.float32),
            jnp.zeros((base - mesh_rows - geo_rows, latent), jnp.float32),
        ],
        axis=0,
    ).astype(jnp.bfloat16)

    def encode(rows_ref, place):
        hidden = half(silu(dot(rows_ref[...], enc_ref[...])))
        lat = half(layer_norm(dot(hidden, enc_out_ref[...])))
        table_ref[pl.ds(place, chunk), :] = half(dot(lat, send_proj_ref[...]))

    start = jnp.where(is_last, base - chunk, base)

    @pl.when(jnp.logical_not(is_last))
    def _():
        encode(first_ref, base)

    encode(second_ref, pl.multiple_of(start + chunk, chunk))

    @pl.when(jnp.logical_not(is_first))
    def _():
        encode(third_ref, pl.multiple_of(start + 2 * chunk, chunk))

    sum_ref[...] = jnp.zeros_like(sum_ref)
    per = EDGE_BLOCK // LANES
    src_shift = jnp.where(is_last, chunk, 0)

    def geometry(block):
        pieces = []
        for k in range(per):
            lane0 = pl.multiple_of(block * EDGE_BLOCK + k * LANES, LANES)
            geo = geo_ref[:, pl.ds(lane0, LANES)].astype(jnp.float32)
            low = mesh_rows % LANES
            square = jnp.concatenate(
                [
                    jnp.zeros((low, LANES), jnp.float32),
                    geo,
                    jnp.zeros((LANES - low - geo_rows, LANES), jnp.float32),
                ],
                axis=0,
            )
            pieces.append(square.T)
        return jnp.concatenate(pieces, axis=0)

    def own_picks(block):
        target = columns(dst_ref, block * per, per)
        lane = lax.broadcasted_iota(jnp.int32, target.shape, 1)
        geo_block = mesh_rows // LANES
        parts = []
        for k in range(base // LANES):
            if k > geo_block:
                parts.append(jnp.zeros(target.shape, jnp.bfloat16))
                continue
            part = jnp.where(target == lane + k * LANES, 1.0, 0.0)
            if k == geo_block:
                part = part + geometry(block)
            parts.append(half(part))
        return jnp.concatenate(parts, axis=1)

    def finish(block, pre):
        act = half(silu(pre))
        lane = lax.broadcasted_iota(jnp.int32, (1, EDGE_BLOCK), 1)
        target = row_of(dst_ref, block * per, per)
        target = jnp.where(block * EDGE_BLOCK + lane < live, target, -1)
        sum_ref[...] += dot(scatter_picks(target, mesh_rows), act)

    def in_order(block, carry):
        pre = dot(own_picks(block), table_ref[0:base, :])
        place = pl.multiple_of(base + block * EDGE_BLOCK, EDGE_BLOCK)
        finish(block, pre + table_ref[pl.ds(place, EDGE_BLOCK), :].astype(jnp.float32))
        return carry

    def at_random(lookup_rows, block, carry):
        source = columns(src_ref, block * per, per) - src_shift
        onehot = jnp.concatenate([own_picks(block), picks(source, lookup_rows)], axis=1)
        finish(block, dot(onehot, table_ref[0 : base + lookup_rows, :]))
        return carry

    blocks = pl.cdiv(live, EDGE_BLOCK)
    ordered = jnp.where(polar, 2, 3) * (chunk // EDGE_BLOCK)
    lax.fori_loop(0, ordered, in_order, 0)

    @pl.when(polar)
    def _():
        lax.fori_loop(ordered, blocks, functools.partial(at_random, 2 * chunk), 0)

    @pl.when(jnp.logical_not(polar))
    def _():
        lax.fori_loop(ordered, blocks, functools.partial(at_random, 3 * chunk), 0)

    total = sum_ref[...]
    high = half(total)
    low = half(total - high.astype(jnp.float32))
    inflow = half(dot(high, msg_ref[...]) + dot(low, msg_ref[...]))
    embed = embed_ref[...]
    node_act = half(silu(dot(embed, node_self_ref[...]) + dot(inflow, node_agg_ref[...])))
    mesh_latent = half(
        embed.astype(jnp.float32) + layer_norm(dot(node_act, node_out_ref[...])) * gain_ref[...]
    )
    latent_ref[...] = mesh_latent
    sender = half(dot(mesh_latent, proc_send_ref[...]))
    pair_ref[0:mesh_rows, :] = sender
    pair_ref[mesh_rows : 2 * mesh_rows, :] = half(dot(mesh_latent, proc_recv_ref[...]))
    padded = -(-mesh_rows // LANES) * LANES
    sender_pad = jnp.concatenate(
        [sender, jnp.zeros((padded - mesh_rows, latent), jnp.bfloat16)], axis=0
    )
    near_slots = near_ref.shape[0]
    for k in range(near_slots):
        out_ref[k * LANES : (k + 1) * LANES, :] = half(
            dot(picks(column(near_ref[k : k + 1, :]), padded), sender_pad)
        )
    for k in range(far_ref.shape[0]):
        out_ref[(near_slots + k) * LANES : (near_slots + k + 1) * LANES, :] = half(
            dot(picks(column(far_ref[k : k + 1, :]), padded), sender_pad)
        )


def edge_start_kernel(src_ref, dst_ref, lat_ref, self_ref, pair_ref, out_ref):
    mesh_rows = pair_ref.shape[0] // 2
    block_rows = 512
    per = block_rows // LANES
    pairs = pair_ref[...]

    def step(block, carry):
        row0 = pl.multiple_of(block * block_rows, block_rows)
        source = columns(src_ref, block * per, per)
        target = columns(dst_ref, block * per, per) + mesh_rows
        lane = lax.broadcasted_iota(jnp.int32, source.shape, 1)
        parts = []
        for first in range(0, 2 * mesh_rows, LANES):
            hit = None
            if first < mesh_rows:
                own = jnp.where(source < mesh_rows, source, -1)
                hit = own == lane + first
            if first + LANES > mesh_rows:
                other = target == lane + first
                hit = other if hit is None else hit | other
            parts.append(half(jnp.where(hit, 1.0, 0.0)))
        onehot = jnp.concatenate(parts, axis=1)
        out_ref[pl.ds(row0, block_rows), :] = dot(
            lat_ref[pl.ds(row0, block_rows), :], self_ref[...]
        ) + dot(onehot, pairs)
        return carry

    lax.fori_loop(0, lat_ref.shape[0] // block_rows, step, 0)


def edge_finish_kernel(
    src_ref,
    dst_ref,
    lat_ref,
    pre_ref,
    near0_ref,
    near1_ref,
    near2_ref,
    far_ref,
    latent_ref,
    edge_out_ref,
    upd_self_ref,
    upd_agg_ref,
    upd_out_ref,
    gain_ref,
    out_ref,
    table_ref,
    sum_ref,
):
    mesh_rows = latent_ref.shape[0]
    block_rows = 512
    per = block_rows // LANES
    near = near0_ref.shape[0]
    table_ref[0:near, :] = near0_ref[...]
    table_ref[near : 2 * near, :] = near1_ref[...]
    table_ref[2 * near : 3 * near, :] = near2_ref[...]
    table_ref[3 * near :, :] = far_ref[...]
    sum_ref[...] = jnp.zeros_like(sum_ref)

    def step(block, carry):
        row0 = pl.multiple_of(block * block_rows, block_rows)
        source = columns(src_ref, block * per, per) - mesh_rows
        pre = pre_ref[pl.ds(row0, block_rows), :] + dot(
            picks(source, table_ref.shape[0]), table_ref[...]
        )
        hidden = half(silu(pre))
        new = half(
            lat_ref[pl.ds(row0, block_rows), :].astype(jnp.float32)
            + layer_norm(dot(hidden, edge_out_ref[...]))
        )
        sum_ref[...] += dot(scatter_picks(row_of(dst_ref, block * per, per), mesh_rows), new)
        return carry

    lax.fori_loop(0, lat_ref.shape[0] // block_rows, step, 0)
    inflow = half(sum_ref[...])
    latent = latent_ref[...]
    act = half(silu(dot(latent, upd_self_ref[...]) + dot(inflow, upd_agg_ref[...])))
    out_ref[...] = half(
        latent.astype(jnp.float32) + layer_norm(dot(act, upd_out_ref[...])) * gain_ref[...]
    )


def body(
    grid_input,
    grid_send,
    grid_edge_src,
    grid_edge_dst,
    edge_count,
    grid_edge_geo,
    mesh_embed,
    mesh_near_send,
    mesh_far_send,
    mesh_edge_src,
    mesh_edge_dst,
    mesh_edge_lat,
    enc_in,
    enc_out,
    send_proj,
    recv_proj,
    geo_proj,
    msg_weight,
    node_self,
    node_agg,
    node_out,
    mesh_gain,
    proc_send,
    proc_recv,
    edge_self,
    edge_out,
    upd_self,
    upd_agg,
    upd_out,
    out_gain,
):
    band_count = lax.axis_size("band")
    sub_count = lax.axis_size("sub")
    slot_cap = grid_send.shape[2]
    near_cap = mesh_near_send.shape[2]
    far_cap = mesh_far_send.shape[1]
    mesh_rows, latent = mesh_embed.shape
    edges = grid_edge_src.shape[0]
    mesh_edges = mesh_edge_src.shape[0]
    wide = 256
    bf16, f32 = jnp.bfloat16, jnp.float32

    sent = 3 * sub_count * slot_cap
    payload = local_call(
        pick_grid_kernel,
        jax.ShapeDtypeStruct((sent, wide), bf16),
        [whole()] * 2,
        flops=2 * sent * grid_input.shape[0] * wide,
        nbytes=2 * wide * (sent + grid_input.shape[0]),
    )(grid_send.reshape(sent // LANES, LANES), grid_input)
    in_sub = lax.all_to_all(
        payload.reshape(3, sub_count, slot_cap, wide), "sub", split_axis=1, concat_axis=1, tiled=True
    )
    arrived = [
        part.reshape(sub_count * slot_cap, wide)
        for part in (shifted(in_sub[0], -1), in_sub[1], shifted(in_sub[2], 1))
    ]

    near_index = mesh_near_send.transpose(1, 0, 2).reshape(-1, LANES)
    far_index = (
        mesh_far_send.reshape(band_count, sub_count, far_cap).transpose(1, 0, 2).reshape(-1, LANES)
    )
    place = jnp.stack([lax.axis_index("band"), jnp.int32(band_count)]).astype(jnp.int32)
    near_total = 3 * sub_count * near_cap
    far_total = band_count * sub_count * far_cap
    mesh_latent, pairs, outgoing = local_call(
        encoder_kernel,
        (
            jax.ShapeDtypeStruct((mesh_rows, latent), bf16),
            jax.ShapeDtypeStruct((2 * mesh_rows, latent), bf16),
            jax.ShapeDtypeStruct((near_total + far_total, latent), bf16),
        ),
        [in_smem()] * 2 + [whole()] * 21,
        scratch=[
            pltpu.VMEM((512 + sent, latent), bf16),
            pltpu.VMEM((wide, latent), bf16),
            pltpu.VMEM((mesh_rows, latent), f32),
        ],
        flops=2 * edges * 2048 * latent,
        nbytes=16 << 20,
    )(
        place,
        edge_count,
        *arrived,
        grid_edge_src.reshape(-1, LANES),
        grid_edge_dst.reshape(-1, LANES),
        grid_edge_geo,
        mesh_embed,
        near_index,
        far_index,
        enc_in,
        enc_out,
        send_proj,
        recv_proj,
        geo_proj,
        msg_weight,
        node_self,
        node_agg,
        node_out,
        mesh_gain.reshape(1, latent),
        proc_send,
        proc_recv,
    )

    mesh_src = mesh_edge_src.reshape(-1, LANES)
    mesh_dst = mesh_edge_dst.reshape(-1, LANES)
    near_out = outgoing[:near_total].reshape(sub_count, 3 * near_cap, latent)
    far_out = outgoing[near_total:].reshape(sub_count, band_count * far_cap, latent)
    near_sub = lax.all_to_all(near_out, "sub", split_axis=0, concat_axis=0, tiled=True).reshape(
        sub_count, 3, near_cap, latent
    )
    near_parts = [
        part.reshape(sub_count * near_cap, latent)
        for part in (shifted(near_sub[:, 0], -1), near_sub[:, 1], shifted(near_sub[:, 2], 1))
    ]
    far_sub = lax.all_to_all(far_out, "sub", split_axis=0, concat_axis=0, tiled=True)
    far_band = lax.all_to_all(
        far_sub.reshape(sub_count, band_count, far_cap, latent).transpose(1, 0, 2, 3),
        "band",
        split_axis=0,
        concat_axis=0,
        tiled=True,
    )
    far_rows = far_band.reshape(far_total, latent)

    pre = local_call(
        edge_start_kernel,
        jax.ShapeDtypeStruct((mesh_edges, latent), f32),
        [whole()] * 5,
        flops=2 * mesh_edges * 1280 * latent,
        nbytes=8 << 20,
    )(mesh_src, mesh_dst, mesh_edge_lat, edge_self, pairs)
    return local_call(
        edge_finish_kernel,
        jax.ShapeDtypeStruct((mesh_rows, latent), bf16),
        [whole()] * 14,
        scratch=[
            pltpu.VMEM((near_total + far_total, latent), bf16),
            pltpu.VMEM((mesh_rows, latent), f32),
        ],
        flops=2 * mesh_edges * 2048 * latent,
        nbytes=12 << 20,
    )(
        mesh_src,
        mesh_dst,
        mesh_edge_lat,
        pre,
        *near_parts,
        far_rows,
        mesh_latent,
        edge_out,
        upd_self,
        upd_agg,
        upd_out,
        out_gain.reshape(1, latent),
    )


def solution(mesh):
    rows = P(("band", "sub"), None)
    blocks = P(("band", "sub"), None, None)
    flat = P(("band", "sub"))
    return jax.shard_map(
        body,
        mesh=mesh,
        in_specs=(
            rows,
            blocks,
            flat,
            flat,
            flat,
            P(None, ("band", "sub")),
            rows,
            blocks,
            rows,
            flat,
            flat,
            rows,
        )
        + (P(),) * 18,
        out_specs=rows,
        check_vma=False,
    )
```

```python
import functools

import jax
import jax.numpy as jnp
from jax import lax
from jax.experimental import pallas as pl
from jax.experimental.pallas import tpu as pltpu
from jax.sharding import PartitionSpec as P

LANES = 128
EDGE_BLOCK = 512
VMEM_BYTES = 28 * 1024 * 1024


def sub_swap(value, step):
    count = lax.axis_size("sub")
    return lax.ppermute(value, "sub", [(t, t ^ step) for t in range(count)])


def mate(band):
    return band ^ 1


def cross(band, count):
    return (((band + 1) ^ 1) - 1) % count


def band_swap(value, partner):
    count = lax.axis_size("band")
    return lax.ppermute(value, "band", [(b, partner(b)) for b in range(count)])


def offsets():
    even = lax.rem(lax.axis_index("band"), 2) == 0
    return (1, jnp.where(even, 2, 0), jnp.where(even, 0, 2))


def sources():
    even = lax.rem(lax.axis_index("band"), 2) == 0
    return (1, jnp.where(even, 0, 2), jnp.where(even, 2, 0))


def layer_norm(values):
    row_mean = jnp.mean(values, axis=-1, keepdims=True)
    centred = values - row_mean
    variance = jnp.mean(centred * centred, axis=-1, keepdims=True)
    return centred * lax.rsqrt(variance + 1e-05)


def silu(values):
    half = 0.5 * values
    return half + half * jnp.tanh(half)


def dot(left, right):
    return jnp.dot(left, right, preferred_element_type=jnp.float32)


def half(values):
    return values.astype(jnp.bfloat16)


def column(row):
    return jnp.broadcast_to(row, (LANES, LANES)).T


def columns(ref, first, count):
    return jnp.concatenate([column(ref[pl.ds(first + k, 1), :]) for k in range(count)], axis=0)


def row_of(ref, first, count):
    return jnp.concatenate([ref[pl.ds(first + k, 1), :] for k in range(count)], axis=1)


def picks(indices, width, offset=0):
    lane = lax.broadcasted_iota(jnp.int32, indices.shape, 1)
    parts = [
        half(jnp.where(indices == lane + (offset + first), 1.0, 0.0))
        for first in range(0, width, LANES)
    ]
    return jnp.concatenate(parts, axis=1)


def scatter_picks(row, height):
    shape = (height, row.shape[1])
    sub = lax.broadcasted_iota(jnp.int32, shape, 0)
    return half(jnp.where(sub == jnp.broadcast_to(row, shape), 1.0, 0.0))


def whole():
    return pl.BlockSpec(memory_space=pltpu.VMEM)


def in_smem():
    return pl.BlockSpec(memory_space=pltpu.SMEM)


def in_hbm():
    return pl.BlockSpec(memory_space=pltpu.HBM)


def local_call(kernel, out_shape, in_specs, scratch=(), flops=0, nbytes=0):
    return pl.pallas_call(
        kernel,
        out_shape=out_shape,
        in_specs=in_specs,
        out_specs=jax.tree.map(lambda _: pl.BlockSpec(memory_space=pltpu.VMEM), out_shape),
        scratch_shapes=list(scratch),
        compiler_params=pltpu.CompilerParams(vmem_limit_bytes=VMEM_BYTES),
        cost_estimate=pl.CostEstimate(flops=flops, bytes_accessed=nbytes, transcendentals=0),
    )


class Fetch:
    def __init__(self, refs, slots, sems):
        self.copies = [
            pltpu.make_async_copy(ref, slots.at[k], sems.at[k]) for k, ref in enumerate(refs)
        ]
        self.slots, self.ready = slots, set()
        for copy in self.copies:
            copy.start()

    def __call__(self, k):
        if k not in self.ready:
            self.copies[k].wait()
            self.ready.add(k)
        return self.slots[k]


def pick_grid_kernel(send_ref, grid_ref, *out_refs):
    width, rows = grid_ref.shape
    wide = out_refs[0].shape[-1]
    me = lax.axis_index("sub")
    index = jnp.concatenate(
        [
            send_ref[offset, pl.ds(me ^ k, 1), :]
            for k in range(len(out_refs))
            for offset in offsets()
        ],
        axis=1,
    )
    for k, out_ref in enumerate(out_refs):
        three = index[:, 3 * LANES * k : 3 * LANES * (k + 1)]
        columns_of = dot(grid_ref[...], scatter_picks(three, rows))
        padded = jnp.concatenate(
            [columns_of, jnp.zeros((wide - width, 3 * LANES), jnp.float32)], axis=0
        )
        for w in range(3):
            out_ref[w] = half(padded[:, w * LANES : (w + 1) * LANES].T)


def encoder_kernel(
    live_ref,
    own0_ref,
    own1_ref,
    own2_ref,
    own3_ref,
    mate_ref,
    cross_ref,
    src_ref,
    dst_ref,
    geo_ref,
    embed_ref,
    near_ref,
    far_ref,
    enc_in_ref,
    geo_proj_ref,
    gain_ref,
    enc_out_ref,
    send_proj_ref,
    recv_proj_ref,
    msg_ref,
    node_self_ref,
    node_agg_ref,
    node_out_ref,
    proc_send_ref,
    proc_recv_ref,
    latent_ref,
    pair_ref,
    out0_ref,
    out1_ref,
    out2_ref,
    out3_ref,
    out_far_ref,
    table_ref,
    enc_ref,
    sum_ref,
    flat_ref,
    slots_ref,
    sems,
):
    weight = Fetch(
        (
            enc_out_ref,
            send_proj_ref,
            recv_proj_ref,
            msg_ref,
            node_self_ref,
            node_agg_ref,
            node_out_ref,
            proc_send_ref,
            proc_recv_ref,
        ),
        slots_ref,
        sems,
    )
    mesh_rows, latent = embed_ref.shape
    subs, cap, wide = mate_ref.shape
    chunk = subs * cap
    base = table_ref.shape[0] - 3 * chunk
    geo_rows = geo_ref.shape[0]
    band, me = lax.axis_index("band"), lax.axis_index("sub")
    is_first = band == 0
    is_last = band == lax.axis_size("band") - 1
    polar = is_first | is_last
    live = live_ref[0]

    enc_ref[...] = jnp.zeros_like(enc_ref)
    enc_ref[0 : enc_in_ref.shape[0], :] = enc_in_ref[...]

    start = jnp.where(is_last, base - chunk, base)
    places = sources()

    def encode(rows, w):
        hidden = half(silu(dot(rows, enc_ref[...])))
        lat = half(layer_norm(dot(hidden, weight(0))))
        sent = half(dot(lat, weight(1)))
        for k in range(subs):
            place = pl.multiple_of(start + places[w] * chunk + (me ^ k) * cap, cap)
            table_ref[pl.ds(place, cap), :] = sent[k * cap : (k + 1) * cap]

    encode(
        jnp.concatenate([ref[0] for ref in (own0_ref, own1_ref, own2_ref, own3_ref)], axis=0), 0
    )
    encode(mate_ref[...].reshape(chunk, wide), 1)

    @pl.when(jnp.logical_not(polar))
    def _():
        encode(cross_ref[...].reshape(chunk, wide), 2)

    table_ref[0:mesh_rows, :] = half(dot(embed_ref[...], weight(2)))
    table_ref[mesh_rows:base, :] = jnp.concatenate(
        [
            geo_proj_ref[...].astype(jnp.float32),
            jnp.zeros((base - mesh_rows - geo_rows, latent), jnp.float32),
        ],
        axis=0,
    ).astype(jnp.bfloat16)

    sum_ref[...] = jnp.zeros_like(sum_ref)
    per = EDGE_BLOCK // LANES
    src_shift = jnp.where(is_last, chunk, 0)

    def geometry(block):
        pieces = []
        for k in range(per):
            lane0 = pl.multiple_of(block * EDGE_BLOCK + k * LANES, LANES)
            geo = geo_ref[:, pl.ds(lane0, LANES)].astype(jnp.float32)
            low = mesh_rows % LANES
            square = jnp.concatenate(
                [
                    jnp.zeros((low, LANES), jnp.float32),
                    geo,
                    jnp.zeros((LANES - low - geo_rows, LANES), jnp.float32),
                ],
                axis=0,
            )
            pieces.append(square.T)
        return jnp.concatenate(pieces, axis=0)

    def own_picks(block):
        target = columns(dst_ref, block * per, per)
        lane = lax.broadcasted_iota(jnp.int32, target.shape, 1)
        geo_block = mesh_rows // LANES
        parts = []
        for k in range(base // LANES):
            if k > geo_block:
                parts.append(jnp.zeros(target.shape, jnp.bfloat16))
                continue
            part = jnp.where(target == lane + k * LANES, 1.0, 0.0)
            if k == geo_block:
                part = part + geometry(block)
            parts.append(half(part))
        return jnp.concatenate(parts, axis=1)

    def finish(block, pre):
        act = half(silu(pre))
        lane = lax.broadcasted_iota(jnp.int32, (1, EDGE_BLOCK), 1)
        target = row_of(dst_ref, block * per, per)
        target = jnp.where(block * EDGE_BLOCK + lane < live, target, -1)
        sum_ref[...] += dot(scatter_picks(target, mesh_rows), act)

    def in_order(block, carry):
        pre = dot(own_picks(block), table_ref[0:base, :])
        place = pl.multiple_of(base + block * EDGE_BLOCK, EDGE_BLOCK)
        finish(block, pre + table_ref[pl.ds(place, EDGE_BLOCK), :].astype(jnp.float32))
        return carry

    def at_random(lookup_rows, block, carry):
        source = columns(src_ref, block * per, per) - src_shift
        onehot = jnp.concatenate([own_picks(block), picks(source, lookup_rows)], axis=1)
        finish(block, dot(onehot, table_ref[0 : base + lookup_rows, :]))
        return carry

    blocks = pl.cdiv(live, EDGE_BLOCK)
    ordered = jnp.where(polar, 2, 3) * (chunk // EDGE_BLOCK)
    lax.fori_loop(0, ordered, in_order, 0)

    @pl.when(polar)
    def _():
        lax.fori_loop(ordered, blocks, functools.partial(at_random, 2 * chunk), 0)

    @pl.when(jnp.logical_not(polar))
    def _():
        lax.fori_loop(ordered, blocks, functools.partial(at_random, 3 * chunk), 0)

    total = sum_ref[...]
    high = half(total)
    low = half(total - high.astype(jnp.float32))
    inflow = half(dot(high, weight(3)) + dot(low, weight(3)))
    embed = embed_ref[...]
    node_act = half(silu(dot(embed, weight(4)) + dot(inflow, weight(5))))
    mesh_latent = half(
        embed.astype(jnp.float32) + layer_norm(dot(node_act, weight(6))) * gain_ref[...]
    )
    latent_ref[...] = mesh_latent
    sender = half(dot(mesh_latent, weight(7)))
    pair_ref[0:mesh_rows, :] = sender
    pair_ref[mesh_rows : 2 * mesh_rows, :] = half(dot(mesh_latent, weight(8)))
    padded = -(-mesh_rows // LANES) * LANES
    sender_pad = jnp.concatenate(
        [sender, jnp.zeros((padded - mesh_rows, latent), jnp.bfloat16)], axis=0
    )
    near = near_ref.shape[2]
    shares = offsets()
    for k, out_ref in enumerate((out0_ref, out1_ref, out2_ref, out3_ref)):
        index = [near_ref[offset, pl.ds(me ^ k, 1), :] for offset in shares]
        index.append(jnp.zeros((1, 4 * near - 3 * near), jnp.int32))
        index = jnp.concatenate(index, axis=1)
        onehot = jnp.concatenate(
            [
                picks(column(index[:, first : first + LANES]), padded)
                for first in range(0, 4 * near, LANES)
            ],
            axis=0,
        )
        out_ref[...] = half(dot(onehot[0 : 3 * near], sender_pad)).reshape(out_ref.shape)
    lanes = latent // LANES
    spread = far_ref.shape[0] * lanes
    for c in range(far_ref.shape[0]):
        rows = dot(picks(column(far_ref[c : c + 1, :]), padded), sender_pad)
        for j in range(lanes):
            flat_ref[pl.ds(c * lanes + j, LANES, stride=spread), :] = rows[
                :, j * LANES : (j + 1) * LANES
            ]
    out_far_ref[...] = half(flat_ref[...])


def edge_start_kernel(src_ref, dst_ref, lat_ref, self_ref, pair_ref, out_ref):
    mesh_rows = pair_ref.shape[0] // 2
    block_rows = 512
    per = block_rows // LANES
    pairs = pair_ref[...]

    def step(block, carry):
        row0 = pl.multiple_of(block * block_rows, block_rows)
        source = columns(src_ref, block * per, per)
        target = columns(dst_ref, block * per, per) + mesh_rows
        lane = lax.broadcasted_iota(jnp.int32, source.shape, 1)
        parts = []
        for first in range(0, 2 * mesh_rows, LANES):
            hit = None
            if first < mesh_rows:
                own = jnp.where(source < mesh_rows, source, -1)
                hit = own == lane + first
            if first + LANES > mesh_rows:
                other = target == lane + first
                hit = other if hit is None else hit | other
            parts.append(half(jnp.where(hit, 1.0, 0.0)))
        onehot = jnp.concatenate(parts, axis=1)
        out_ref[pl.ds(row0, block_rows), :] = dot(
            lat_ref[pl.ds(row0, block_rows), :], self_ref[...]
        ) + dot(onehot, pairs)
        return carry

    lax.fori_loop(0, lat_ref.shape[0] // block_rows, step, 0)


def edge_finish_kernel(
    src_ref,
    dst_ref,
    lat_ref,
    pre_ref,
    own0_ref,
    own1_ref,
    own2_ref,
    own3_ref,
    mate_ref,
    cross_ref,
    far_ref,
    latent_ref,
    gain_ref,
    edge_out_ref,
    upd_self_ref,
    upd_agg_ref,
    upd_out_ref,
    out_ref,
    table_ref,
    sum_ref,
    flat_ref,
    slots_ref,
    sems,
):
    weight = Fetch((edge_out_ref, upd_self_ref, upd_agg_ref, upd_out_ref), slots_ref, sems)
    mesh_rows, latent = latent_ref.shape
    block_rows = 512
    per = block_rows // LANES
    subs, near, _ = mate_ref.shape
    near_total = 3 * subs * near
    me = lax.axis_index("sub")
    owns = (own0_ref, own1_ref, own2_ref, own3_ref)
    for w, offset in enumerate(sources()):
        for k in range(subs):
            rows = owns[k][0] if w == 0 else (mate_ref, cross_ref)[w - 1][k]
            place = pl.multiple_of((offset * subs + (me ^ k)) * near, near)
            table_ref[pl.ds(place, near), :] = rows
    lanes = latent // LANES
    devices = far_ref.shape[0] // (2 * lanes)
    flat_ref[...] = far_ref[...].astype(jnp.float32)
    for c in range(2):
        table_ref[pl.ds(near_total + c * devices, devices), :] = half(
            jnp.concatenate(
                [
                    flat_ref[pl.ds(c * lanes + j, devices, stride=2 * lanes), :]
                    for j in range(lanes)
                ],
                axis=1,
            )
        )
    edge_out = weight(0)
    sum_ref[...] = jnp.zeros_like(sum_ref)

    def step(block, carry):
        row0 = pl.multiple_of(block * block_rows, block_rows)
        source = columns(src_ref, block * per, per) - mesh_rows
        far = source - near_total
        far = near_total + (far & 1) * devices + (far >> 1)
        source = jnp.where(source < near_total, source, far)
        pre = pre_ref[pl.ds(row0, block_rows), :] + dot(
            picks(source, table_ref.shape[0]), table_ref[...]
        )
        hidden = half(silu(pre))
        new = half(
            lat_ref[pl.ds(row0, block_rows), :].astype(jnp.float32)
            + layer_norm(dot(hidden, edge_out))
        )
        sum_ref[...] += dot(scatter_picks(row_of(dst_ref, block * per, per), mesh_rows), new)
        return carry

    lax.fori_loop(0, lat_ref.shape[0] // block_rows, step, 0)
    inflow = half(sum_ref[...])
    latent = latent_ref[...]
    act = half(silu(dot(latent, weight(1)) + dot(inflow, weight(2))))
    out_ref[...] = half(
        latent.astype(jnp.float32) + layer_norm(dot(act, weight(3))) * gain_ref[...]
    )


def body(
    grid_input,
    grid_send,
    grid_edge_src,
    grid_edge_dst,
    edge_count,
    grid_edge_geo,
    mesh_embed,
    mesh_near_send,
    mesh_far_send,
    mesh_edge_src,
    mesh_edge_dst,
    mesh_edge_lat,
    enc_in,
    enc_out,
    send_proj,
    recv_proj,
    geo_proj,
    msg_weight,
    node_self,
    node_agg,
    node_out,
    mesh_gain,
    proc_send,
    proc_recv,
    edge_self,
    edge_out,
    upd_self,
    upd_agg,
    upd_out,
    out_gain,
):
    sub_count = lax.axis_size("sub")
    devices = lax.axis_size("band") * sub_count
    slot_cap = grid_send.shape[2]
    near_cap = mesh_near_send.shape[2]
    far_cap = mesh_far_send.shape[1]
    mesh_rows, latent = mesh_embed.shape
    edges = grid_edge_src.shape[0]
    mesh_edges = mesh_edge_src.shape[0]
    wide = 256
    bf16, f32 = jnp.bfloat16, jnp.float32

    def exchange(parts):
        arrived = [parts[0]] + [sub_swap(parts[k], k) for k in range(1, sub_count)]
        mates = band_swap(jnp.stack([part[1] for part in arrived]), mate)
        crosses = band_swap(
            jnp.stack([part[2] for part in arrived]),
            functools.partial(cross, count=lax.axis_size("band")),
        )
        return *arrived, mates, crosses

    sent = 3 * sub_count * slot_cap
    parts = local_call(
        pick_grid_kernel,
        (jax.ShapeDtypeStruct((3, slot_cap, wide), bf16),) * sub_count,
        [whole()] * 2,
        flops=2 * sent * grid_input.shape[0] * wide,
        nbytes=2 * wide * (sent + grid_input.shape[0]),
    )(grid_send, grid_input.T)
    arrived = exchange(parts)

    far_total = devices * far_cap
    mesh_latent, pairs, *near_parts, far_out = local_call(
        encoder_kernel,
        (
            jax.ShapeDtypeStruct((mesh_rows, latent), bf16),
            jax.ShapeDtypeStruct((2 * mesh_rows, latent), bf16),
        )
        + (jax.ShapeDtypeStruct((3, near_cap, latent), bf16),) * sub_count
        + (jax.ShapeDtypeStruct((far_total * latent // LANES, LANES), bf16),),
        [in_smem()] + [whole()] * 15 + [in_hbm()] * 9,
        scratch=[
            pltpu.VMEM((512 + sent, latent), bf16),
            pltpu.VMEM((wide, latent), bf16),
            pltpu.VMEM((mesh_rows, latent), f32),
            pltpu.VMEM((far_total * latent // LANES, LANES), f32),
            pltpu.VMEM((9, latent, latent), bf16),
            pltpu.SemaphoreType.DMA((9,)),
        ],
        flops=2 * edges * 2048 * latent,
        nbytes=16 << 20,
    )(
        edge_count,
        *arrived,
        grid_edge_src.reshape(-1, LANES),
        grid_edge_dst.reshape(-1, LANES),
        grid_edge_geo,
        mesh_embed,
        mesh_near_send,
        mesh_far_send.T,
        enc_in,
        geo_proj,
        mesh_gain.reshape(1, latent),
        enc_out,
        send_proj,
        recv_proj,
        msg_weight,
        node_self,
        node_agg,
        node_out,
        proc_send,
        proc_recv,
    )

    mesh_src = mesh_edge_src.reshape(-1, LANES)
    mesh_dst = mesh_edge_dst.reshape(-1, LANES)
    near_arrived = exchange(near_parts)
    far_rows = lax.all_to_all(
        far_out.reshape(devices, -1, LANES),
        ("band", "sub"),
        split_axis=0,
        concat_axis=0,
        tiled=True,
    ).reshape(-1, LANES)

    pre = local_call(
        edge_start_kernel,
        jax.ShapeDtypeStruct((mesh_edges, latent), f32),
        [whole()] * 5,
        flops=2 * mesh_edges * 1280 * latent,
        nbytes=8 << 20,
    )(mesh_src, mesh_dst, mesh_edge_lat, edge_self, pairs)
    near_total = 3 * sub_count * near_cap
    return local_call(
        edge_finish_kernel,
        jax.ShapeDtypeStruct((mesh_rows, latent), bf16),
        [whole()] * 13 + [in_hbm()] * 4,
        scratch=[
            pltpu.VMEM((near_total + far_total, latent), bf16),
            pltpu.VMEM((mesh_rows, latent), f32),
            pltpu.VMEM((far_total * latent // LANES, LANES), f32),
            pltpu.VMEM((4, latent, latent), bf16),
            pltpu.SemaphoreType.DMA((4,)),
        ],
        flops=2 * mesh_edges * 2048 * latent,
        nbytes=12 << 20,
    )(
        mesh_src,
        mesh_dst,
        mesh_edge_lat,
        pre,
        *near_arrived,
        far_rows,
        mesh_latent,
        out_gain.reshape(1, latent),
        edge_out,
        upd_self,
        upd_agg,
        upd_out,
    )


def solution(mesh):
    rows = P(("band", "sub"), None)
    blocks = P(("band", "sub"), None, None)
    flat = P(("band", "sub"))
    return jax.shard_map(
        body,
        mesh=mesh,
        in_specs=(
            rows,
            blocks,
            flat,
            flat,
            flat,
            P(None, ("band", "sub")),
            rows,
            blocks,
            rows,
            flat,
            flat,
            rows,
        )
        + (P(),) * 18,
        out_specs=rows,
        check_vma=False,
    )
```

```python
import functools

import jax
import jax.numpy as jnp
from jax import lax
from jax.experimental import pallas as pl
from jax.experimental.pallas import tpu as pltpu
from jax.sharding import PartitionSpec as P

LANES = 128
EDGE_BLOCK = 512
PAIR = 2 * EDGE_BLOCK
VMEM_BYTES = 24 * 1024 * 1024
VMEM_ALL = 60 * 1024 * 1024
START_FLOPS = 2 * 10**9
START_BYTES = 8 << 20


def sub_swap(value, step):
    count = lax.axis_size("sub")
    return lax.ppermute(value, "sub", [(t, t ^ step) for t in range(count)])


def mate(band):
    return band ^ 1


def cross(band, count):
    return (((band + 1) ^ 1) - 1) % count


def band_swap(value, partner):
    count = lax.axis_size("band")
    return lax.ppermute(value, "band", [(b, partner(b)) for b in range(count)])


def offsets():
    even = lax.rem(lax.axis_index("band"), 2) == 0
    return (1, jnp.where(even, 2, 0), jnp.where(even, 0, 2))


def sources():
    even = lax.rem(lax.axis_index("band"), 2) == 0
    return (1, jnp.where(even, 0, 2), jnp.where(even, 2, 0))


def layer_norm(values):
    row_mean = jnp.mean(values, axis=-1, keepdims=True)
    centred = values - row_mean
    variance = jnp.mean(centred * centred, axis=-1, keepdims=True)
    return centred * lax.rsqrt(variance + 1e-05)


def silu(values):
    half = 0.5 * values
    return half + half * jnp.tanh(half)


def dot(left, right):
    return jnp.dot(left, right, preferred_element_type=jnp.float32)


def half(values):
    return values.astype(jnp.bfloat16)


def column(row):
    return jnp.broadcast_to(row, (LANES, LANES)).T


def row_of(ref, first, count):
    return jnp.concatenate([ref[pl.ds(first + k, 1), :] for k in range(count)], axis=1)


def spread(rows, places):
    lanes = sum(1 for _ in places) * LANES
    lane = lax.broadcasted_iota(jnp.int32, (8, lanes), 1)
    row = lax.broadcasted_iota(jnp.int32, (8, lanes), 0)
    factors = jnp.zeros((8, lanes), jnp.float32)
    for k, entries in enumerate(places):
        for index, low, high, factor in entries:
            here = (row == index) & (lane >= k * LANES + low) & (lane < k * LANES + high)
            factors = jnp.where(here, factor, factors)
    return dot(half(rows.T), half(factors))


def digits(row):
    return [(row >> 7).astype(jnp.float32), (row & (LANES - 1)).astype(jnp.float32)]


def index_entry(first):
    return [(first, 0, LANES, float(LANES)), (first + 1, 0, LANES, 1.0)]


def lanes_of(indices):
    return lax.broadcasted_iota(jnp.int32, indices.shape, 1).astype(jnp.float32)


def picks(indices, width):
    lane = lanes_of(indices)
    indices = indices.astype(jnp.float32)
    parts = [
        half(jnp.where(indices == lane + float(first), 1.0, 0.0))
        for first in range(0, width, LANES)
    ]
    return jnp.concatenate(parts, axis=1)


def scatter_picks(row, height):
    shape = (height, row.shape[1])
    sub = lax.broadcasted_iota(jnp.int32, shape, 0)
    return half(jnp.where(sub == jnp.broadcast_to(row, shape), 1.0, 0.0))


def whole():
    return pl.BlockSpec(memory_space=pltpu.VMEM)


def in_smem():
    return pl.BlockSpec(memory_space=pltpu.SMEM)


def in_hbm():
    return pl.BlockSpec(memory_space=pltpu.HBM)


def local_call(
    kernel, out_shape, in_specs, scratch=(), flops=0, nbytes=0, out_specs=None, vmem=VMEM_BYTES
):
    return pl.pallas_call(
        kernel,
        out_shape=out_shape,
        in_specs=in_specs,
        out_specs=out_specs or jax.tree.map(lambda _: whole(), out_shape),
        scratch_shapes=list(scratch),
        compiler_params=pltpu.CompilerParams(vmem_limit_bytes=vmem),
        cost_estimate=pl.CostEstimate(flops=flops, bytes_accessed=nbytes, transcendentals=0),
    )


class Fetch:
    def __init__(self, refs, slots, sems):
        self.copies = [
            pltpu.make_async_copy(ref, slots.at[k], sems.at[k]) for k, ref in enumerate(refs)
        ]
        self.slots, self.ready = slots, set()
        for copy in self.copies:
            copy.start()

    def __call__(self, k):
        if k not in self.ready:
            self.copies[k].wait()
            self.ready.add(k)
        return self.slots.at[k]


def pick_grid_kernel(send_ref, grid_ref, *refs):
    out_refs, sum_ref = refs[:-1], refs[-1]
    width, rows = grid_ref.shape
    wide = out_refs[0].shape[-1]
    me = lax.axis_index("sub")
    part = pl.program_id(0)
    index = jnp.concatenate(
        [
            send_ref[offset, pl.ds(me ^ k, 1), :]
            for k in range(len(out_refs))
            for offset in offsets()
        ],
        axis=1,
    )
    picked = dot(grid_ref[...], scatter_picks(index - part * rows, rows))

    @pl.when(part == 0)
    def _():
        sum_ref[0:width, :] = picked
        sum_ref[width:, :] = jnp.zeros((wide - width, picked.shape[1]), jnp.float32)

    @pl.when(part > 0)
    def _():
        sum_ref[0:width, :] += picked

    @pl.when(part == pl.num_programs(0) - 1)
    def _():
        for k, out_ref in enumerate(out_refs):
            for w in range(3):
                first = (3 * k + w) * LANES
                out_ref[w] = half(sum_ref[:, first : first + LANES].T)


def prepare_grid_kernel(
    live_ref,
    src_ref,
    dst_ref,
    geo_ref,
    embed_ref,
    recv_proj_ref,
    geo_proj_ref,
    node_self_ref,
    place_ref,
    own_ref,
    node_ref,
    table_ref,
):
    mesh_rows, latent = embed_ref.shape
    base = table_ref.shape[0]
    geo_rows = geo_ref.shape[0]
    received = 3 * lax.axis_size("sub") * LANES
    is_last = lax.axis_index("band") == lax.axis_size("band") - 1
    src_shift = jnp.where(is_last, received // 3, 0)
    node_ref[...] = dot(embed_ref[...], node_self_ref[...])
    table_ref[0:mesh_rows, :] = half(dot(embed_ref[...], recv_proj_ref[...]))
    table_ref[mesh_rows:base, :] = half(
        jnp.concatenate(
            [
                geo_proj_ref[...].astype(jnp.float32),
                jnp.zeros((base - mesh_rows - geo_rows, latent), jnp.float32),
            ],
            axis=0,
        )
    )
    low = mesh_rows % LANES
    places = [
        index_entry(0),
        index_entry(2),
        [(4 + k, low + k, low + k + 1, 1.0) for k in range(geo_rows)],
    ]
    per = EDGE_BLOCK // LANES

    def step(block, carry):
        row0 = pl.multiple_of(block * EDGE_BLOCK, EDGE_BLOCK)
        rows = jnp.concatenate(
            digits(row_of(src_ref, block * per, per) - src_shift)
            + digits(row_of(dst_ref, block * per, per))
            + [geo_ref[:, pl.ds(row0, EDGE_BLOCK)].astype(jnp.float32)],
            axis=0,
        )
        wide = spread(rows, places)
        place_ref[pl.ds(row0, EDGE_BLOCK), :] = wide[:, 0:LANES]
        target = wide[:, LANES : 2 * LANES]
        lane = lanes_of(target)
        parts = []
        for k in range(base // LANES):
            part = jnp.where(target == lane + float(k * LANES), 1.0, 0.0)
            if k == mesh_rows // LANES:
                part = part + wide[:, 2 * LANES :]
            parts.append(half(part))
        own = dot(jnp.concatenate(parts, axis=1), table_ref[...])
        own_ref[pl.ds(row0, EDGE_BLOCK), :] = half(own)
        return carry

    lax.fori_loop(0, pl.cdiv(live_ref[0], PAIR) * (PAIR // EDGE_BLOCK), step, 0)


def encode_rows(rows, enc_in, enc_out, send_proj):
    hidden = half(silu(dot(rows, enc_in)))
    lat = half(layer_norm(dot(hidden, enc_out)))
    return half(dot(lat, send_proj))


def padded_rows(ref, rows):
    values = ref[...].astype(jnp.float32)
    zeros = jnp.zeros((rows - values.shape[0], values.shape[1]), jnp.float32)
    return half(jnp.concatenate([values, zeros], axis=0))


def encode_own_kernel(
    own0_ref, own1_ref, own2_ref, own3_ref, enc_in_ref, enc_out_ref, send_proj_ref, out_ref
):
    owns = (own0_ref, own1_ref, own2_ref, own3_ref)
    cap, wide = own0_ref.shape[1:]
    me = lax.axis_index("sub")
    sent = encode_rows(
        jnp.concatenate([ref[0] for ref in owns], axis=0),
        padded_rows(enc_in_ref, wide),
        enc_out_ref[...],
        send_proj_ref[...],
    )
    for k in range(len(owns)):
        out_ref[pl.ds(pl.multiple_of((me ^ k) * cap, cap), cap), :] = sent[
            k * cap : (k + 1) * cap
        ]


def encoder_kernel(
    live_ref,
    own_rows_ref,
    mate_ref,
    cross_ref,
    place_ref,
    own_ref,
    dst_ref,
    embed_ref,
    node_ref,
    near_ref,
    far_ref,
    enc_in_ref,
    gain_ref,
    enc_out_ref,
    send_proj_ref,
    msg_ref,
    node_agg_ref,
    node_out_ref,
    proc_send_ref,
    proc_recv_ref,
    latent_ref,
    pair_ref,
    out0_ref,
    out1_ref,
    out2_ref,
    out3_ref,
    out_far_ref,
    table_ref,
    sum_ref,
    flat_ref,
    act_ref,
    slots_ref,
    sems,
):
    weight = Fetch(
        (
            enc_out_ref,
            send_proj_ref,
            msg_ref,
            node_agg_ref,
            node_out_ref,
            proc_send_ref,
            proc_recv_ref,
        ),
        slots_ref,
        sems,
    )
    mesh_rows, latent = embed_ref.shape
    subs, cap, wide = mate_ref.shape
    chunk = subs * cap
    band, me = lax.axis_index("band"), lax.axis_index("sub")
    is_first = band == 0
    is_last = band == lax.axis_size("band") - 1
    polar = is_first | is_last
    live = live_ref[0]
    enc_in = padded_rows(enc_in_ref, wide)

    start = jnp.where(is_last, -chunk, 0)
    _, mate_place, cross_place = sources()
    table_ref[pl.ds(pl.multiple_of(start + chunk, chunk), chunk), :] = own_rows_ref[...]

    def encode(ref, offset):
        sent = encode_rows(ref[...].reshape(chunk, wide), enc_in, weight(0)[...], weight(1)[...])
        for k in range(subs):
            place = pl.multiple_of(start + offset * chunk + (me ^ k) * cap, cap)
            table_ref[pl.ds(place, cap), :] = sent[k * cap : (k + 1) * cap]

    encode(mate_ref, mate_place)

    @pl.when(jnp.logical_not(polar))
    def _():
        encode(cross_ref, cross_place)

    sum_ref[...] = jnp.zeros_like(sum_ref)

    def scatter(pair):
        lane = lax.broadcasted_iota(jnp.int32, (1, PAIR), 1)
        target = row_of(dst_ref, pair * (PAIR // LANES), PAIR // LANES)
        target = jnp.where(pair * PAIR + lane < live, target, -1)
        sum_ref[...] += dot(scatter_picks(target, mesh_rows), act_ref[...])

    act_ref[...] = half(
        silu(table_ref[0:PAIR, :].astype(jnp.float32) + own_ref[0:PAIR, :].astype(jnp.float32))
    )
    scatter(0)

    def edges(lookup_rows):
        def step(pair, carry):
            for k in range(PAIR // EDGE_BLOCK):
                row0 = pl.multiple_of(pair * PAIR + k * EDGE_BLOCK, EDGE_BLOCK)
                onehot = picks(place_ref[pl.ds(row0, EDGE_BLOCK), :], lookup_rows)
                pre = dot(onehot, table_ref[0:lookup_rows, :]) + own_ref[
                    pl.ds(row0, EDGE_BLOCK), :
                ].astype(jnp.float32)
                act_ref[k * EDGE_BLOCK : (k + 1) * EDGE_BLOCK, :] = half(silu(pre))
            scatter(pair)
            return carry

        lax.fori_loop(1, pl.cdiv(live, PAIR), step, 0)

    @pl.when(polar)
    def _():
        edges(2 * chunk)

    @pl.when(jnp.logical_not(polar))
    def _():
        edges(3 * chunk)

    total = sum_ref[...]
    high = half(total)
    low = half(total - high.astype(jnp.float32))
    inflow = half(dot(high, weight(2)[...]) + dot(low, weight(2)[...]))
    embed = embed_ref[...]
    node_act = half(silu(node_ref[...] + dot(inflow, weight(3)[...])))
    mesh_latent = half(
        embed.astype(jnp.float32) + layer_norm(dot(node_act, weight(4)[...])) * gain_ref[...]
    )
    latent_ref[...] = mesh_latent
    sender = half(dot(mesh_latent, weight(5)[...]))
    pair_ref[0:mesh_rows, :] = sender
    pair_ref[mesh_rows : 2 * mesh_rows, :] = half(dot(mesh_latent, weight(6)[...]))
    padded = -(-mesh_rows // LANES) * LANES
    sender_pad = jnp.concatenate(
        [sender, jnp.zeros((padded - mesh_rows, latent), jnp.bfloat16)], axis=0
    )
    near = near_ref.shape[2]
    shares = offsets()
    for k, out_ref in enumerate((out0_ref, out1_ref, out2_ref, out3_ref)):
        index = [near_ref[offset, pl.ds(me ^ k, 1), :] for offset in shares]
        index.append(jnp.zeros((1, 4 * near - 3 * near), jnp.int32))
        index = jnp.concatenate(index, axis=1)
        onehot = jnp.concatenate(
            [
                picks(column(index[:, first : first + LANES]), padded)
                for first in range(0, 4 * near, LANES)
            ],
            axis=0,
        )
        out_ref[...] = half(dot(onehot[0 : 3 * near], sender_pad)).reshape(out_ref.shape)
    lanes = latent // LANES
    spread = far_ref.shape[0] * lanes
    for c in range(far_ref.shape[0]):
        rows = dot(picks(column(far_ref[c : c + 1, :]), padded), sender_pad)
        for j in range(lanes):
            flat_ref[pl.ds(c * lanes + j, LANES, stride=spread), :] = rows[
                :, j * LANES : (j + 1) * LANES
            ]
    out_far_ref[...] = half(flat_ref[...])


def edge_start_kernel(
    src_ref,
    dst_ref,
    pair_ref,
    lat_hbm,
    self_hbm,
    pre_hbm,
    place_hbm,
    lat_ref,
    self_ref,
    pre_ref,
    place_ref,
    read_sems,
    write_sems,
):
    mesh_rows = pair_ref.shape[0] // 2
    subs = lax.axis_size("sub")
    devices = lax.axis_size("band") * subs
    near_total = 3 * subs * (LANES // 2)
    blocks = lat_ref.shape[0] // EDGE_BLOCK
    per = EDGE_BLOCK // LANES
    spans = [pl.ds(block * EDGE_BLOCK, EDGE_BLOCK) for block in range(blocks)]
    weight = pltpu.make_async_copy(self_hbm, self_ref, read_sems.at[blocks])
    reads = [
        pltpu.make_async_copy(lat_hbm.at[span], lat_ref.at[span], read_sems.at[k])
        for k, span in enumerate(spans)
    ]
    writes = []
    for copy in [weight, *reads]:
        copy.start()
    places = [index_entry(0), index_entry(2), index_entry(4)]
    for block, span in enumerate(spans):
        source = row_of(src_ref, block * per, per)
        target = row_of(dst_ref, block * per, per)
        other = source - mesh_rows
        far = other - near_total
        far = near_total + (far & 1) * devices + (far >> 1)
        rows = jnp.concatenate(
            digits(jnp.where(source < mesh_rows, source, -1))
            + digits(target + mesh_rows)
            + digits(jnp.where(other < near_total, other, far))
            + [jnp.zeros((2, EDGE_BLOCK), jnp.float32)],
            axis=0,
        )
        wide = spread(rows, places)
        own, mine = wide[:, 0:LANES], wide[:, LANES : 2 * LANES]
        place_ref[span, :] = wide[:, 2 * LANES :]
        lane = lanes_of(own)
        parts = []
        for first in range(0, 2 * mesh_rows, LANES):
            hit = None
            if first < mesh_rows:
                hit = own == lane + float(first)
            if first + LANES > mesh_rows:
                match = mine == lane + float(first)
                hit = match if hit is None else hit | match
            parts.append(half(jnp.where(hit, 1.0, 0.0)))
        picked = dot(jnp.concatenate(parts, axis=1), pair_ref[...])
        if block == 0:
            weight.wait()
        reads[block].wait()
        pre_ref[span, :] = half(picked + dot(lat_ref[span, :], self_ref[...]))
        for j, (ref, hbm) in enumerate(((pre_ref, pre_hbm), (place_ref, place_hbm))):
            writes.append(
                pltpu.make_async_copy(ref.at[span], hbm.at[span], write_sems.at[2 * block + j])
            )
            writes[-1].start()
    for copy in writes:
        copy.wait()


def edge_finish_kernel(
    dst_ref,
    far_ref,
    latent_ref,
    gain_ref,
    pre_hbm,
    place_hbm,
    lat_hbm,
    own0_hbm,
    own1_hbm,
    own2_hbm,
    own3_hbm,
    mate_hbm,
    cross_hbm,
    edge_out_ref,
    upd_self_ref,
    upd_agg_ref,
    upd_out_ref,
    out_ref,
    table_ref,
    flat_ref,
    new_ref,
    pre_ref,
    place_ref,
    lat_ref,
    slots_ref,
    sems,
    table_sems,
    block_sems,
):
    mesh_rows, latent = latent_ref.shape
    blocks = lat_ref.shape[0] // EDGE_BLOCK
    spans = [pl.ds(block * EDGE_BLOCK, EDGE_BLOCK) for block in range(blocks)]
    subs, near, _ = mate_hbm.shape
    near_total = 3 * subs * near
    me = lax.axis_index("sub")
    owns = (own0_hbm, own1_hbm, own2_hbm, own3_hbm)
    rows = []
    for w, offset in enumerate(sources()):
        for k in range(subs):
            source = owns[k].at[0] if w == 0 else (mate_hbm, cross_hbm)[w - 1].at[k]
            place = pl.multiple_of((offset * subs + (me ^ k)) * near, near)
            rows.append(
                pltpu.make_async_copy(
                    source, table_ref.at[pl.ds(place, near)], table_sems.at[w * subs + k]
                )
            )
    moved = ((pre_hbm, pre_ref), (place_hbm, place_ref), (lat_hbm, lat_ref))
    reads = [
        [
            pltpu.make_async_copy(hbm.at[span], ref.at[span], block_sems.at[3 * k + j])
            for j, (hbm, ref) in enumerate(moved)
        ]
        for k, span in enumerate(spans)
    ]
    for copy in rows + reads[0]:
        copy.start()
    weight = Fetch((edge_out_ref, upd_self_ref, upd_agg_ref, upd_out_ref), slots_ref, sems)
    for block in reads[1:]:
        for copy in block:
            copy.start()
    lanes = latent // LANES
    devices = far_ref.shape[0] // (2 * lanes)
    flat_ref[...] = far_ref[...].astype(jnp.float32)
    for c in range(2):
        table_ref[pl.ds(near_total + c * devices, devices), :] = half(
            jnp.concatenate(
                [
                    flat_ref[pl.ds(c * lanes + j, devices, stride=2 * lanes), :]
                    for j in range(lanes)
                ],
                axis=1,
            )
        )
    for copy in rows:
        copy.wait()
    edge_out = weight(0)[...]
    upd_self = dot(latent_ref[...], weight(1)[...])

    def gathered(block):
        span = spans[block]
        for copy in reads[block]:
            copy.wait()
        return pre_ref[span, :].astype(jnp.float32) + dot(
            picks(place_ref[span, :], table_ref.shape[0]), table_ref[...]
        )

    def settle(block, pre):
        span = spans[block]
        out = layer_norm(dot(half(silu(pre)), edge_out))
        new_ref[span, :] = half(lat_ref[span, :].astype(jnp.float32) + out)

    pre = gathered(0)
    for block in range(1, blocks):
        later = gathered(block)
        settle(block - 1, pre)
        pre = later
    settle(blocks - 1, pre)
    target = row_of(dst_ref, 0, lat_ref.shape[0] // LANES)
    inflow = half(dot(scatter_picks(target, mesh_rows), new_ref[...]))
    latent = latent_ref[...]
    act = half(silu(upd_self + dot(inflow, weight(2)[...])))
    out_ref[...] = half(
        latent.astype(jnp.float32) + layer_norm(dot(act, weight(3)[...])) * gain_ref[...]
    )


def body(
    grid_input,
    grid_send,
    grid_edge_src,
    grid_edge_dst,
    edge_count,
    grid_edge_geo,
    mesh_embed,
    mesh_near_send,
    mesh_far_send,
    mesh_edge_src,
    mesh_edge_dst,
    mesh_edge_lat,
    enc_in,
    enc_out,
    send_proj,
    recv_proj,
    geo_proj,
    msg_weight,
    node_self,
    node_agg,
    node_out,
    mesh_gain,
    proc_send,
    proc_recv,
    edge_self,
    edge_out,
    upd_self,
    upd_agg,
    upd_out,
    out_gain,
):
    sub_count = lax.axis_size("sub")
    devices = lax.axis_size("band") * sub_count
    slot_cap = grid_send.shape[2]
    near_cap = mesh_near_send.shape[2]
    far_cap = mesh_far_send.shape[1]
    mesh_rows, latent = mesh_embed.shape
    edges = grid_edge_src.shape[0]
    mesh_edges = mesh_edge_src.shape[0]
    wide = 256
    bf16, f32 = jnp.bfloat16, jnp.float32

    def across_subs(parts):
        return [parts[0]] + [sub_swap(parts[k], k) for k in range(1, sub_count)]

    def across_bands(arrived):
        mates = band_swap(jnp.stack([part[1] for part in arrived]), mate)
        crosses = band_swap(
            jnp.stack([part[2] for part in arrived]),
            functools.partial(cross, count=lax.axis_size("band")),
        )
        return mates, crosses

    def shape(*dims, dtype=bf16):
        return jax.ShapeDtypeStruct(dims, dtype)

    received = sub_count * slot_cap
    halves = grid_input.shape[0] // 2
    parts = pl.pallas_call(
        pick_grid_kernel,
        grid=(2,),
        out_shape=(shape(3, slot_cap, wide),) * sub_count,
        in_specs=[
            pl.BlockSpec(grid_send.shape, lambda i: (0, 0, 0)),
            pl.BlockSpec((grid_input.shape[1], halves), lambda i: (0, i)),
        ],
        out_specs=(pl.BlockSpec((3, slot_cap, wide), lambda i: (0, 0, 0)),) * sub_count,
        scratch_shapes=[pltpu.VMEM((wide, 3 * received), f32)],
        compiler_params=pltpu.CompilerParams(vmem_limit_bytes=VMEM_ALL),
        cost_estimate=pl.CostEstimate(
            flops=6 * received * grid_input.shape[0] * wide,
            bytes_accessed=2 * wide * (3 * received + grid_input.shape[0]),
            transcendentals=0,
        ),
    )(grid_send, grid_input.T)
    arrived = across_subs(parts)

    far_total = devices * far_cap
    others = 3 * sub_count * near_cap + far_total
    blocks = mesh_edges // EDGE_BLOCK
    edge_src, _ = lax.optimization_barrier((grid_edge_src, parts[0]))
    edge_dst = grid_edge_dst.reshape(-1, LANES)
    mesh_src = mesh_edge_src.reshape(-1, LANES)
    mesh_dst = mesh_edge_dst.reshape(-1, LANES)
    place, own, node = local_call(
        prepare_grid_kernel,
        (
            shape(edges, LANES, dtype=f32),
            shape(edges, latent),
            shape(mesh_rows, latent, dtype=f32),
        ),
        [in_smem()] + [whole()] * 7,
        scratch=[pltpu.VMEM((384, latent), bf16)],
        flops=2 * edges * 1024 * latent,
        nbytes=16 << 20,
    )(
        edge_count,
        edge_src.reshape(-1, LANES),
        edge_dst,
        grid_edge_geo,
        mesh_embed,
        recv_proj,
        geo_proj,
        node_self,
    )

    arrived, place, own, node = lax.optimization_barrier((arrived, place, own, node))
    mates, crosses = across_bands(arrived)
    own_rows = local_call(
        encode_own_kernel,
        shape(received, latent),
        [whole()] * 7,
        flops=2 * received * 1280 * latent,
        nbytes=3 << 20,
    )(*arrived, enc_in, enc_out, send_proj)

    mesh_latent, pairs, *near_parts, far_out = local_call(
        encoder_kernel,
        (
            shape(mesh_rows, latent),
            shape(2 * mesh_rows, latent),
        )
        + (shape(3, near_cap, latent),) * sub_count
        + (shape(far_total * latent // LANES, LANES),),
        [in_smem()] + [whole()] * 12 + [in_hbm()] * 7,
        scratch=[
            pltpu.VMEM((3 * received, latent), bf16),
            pltpu.VMEM((mesh_rows, latent), f32),
            pltpu.VMEM((far_total * latent // LANES, LANES), f32),
            pltpu.VMEM((PAIR, latent), bf16),
            pltpu.VMEM((7, latent, latent), bf16),
            pltpu.SemaphoreType.DMA((7,)),
        ],
        flops=2 * edges * 2048 * latent,
        nbytes=16 << 20,
    )(
        edge_count,
        own_rows,
        mates,
        crosses,
        place,
        own,
        edge_dst,
        mesh_embed,
        node,
        mesh_near_send,
        mesh_far_send.T,
        enc_in,
        mesh_gain.reshape(1, latent),
        enc_out,
        send_proj,
        msg_weight,
        node_agg,
        node_out,
        proc_send,
        proc_recv,
    )

    near_arrived = across_subs(near_parts)
    far_rows = lax.all_to_all(
        far_out.reshape(devices, -1, LANES),
        ("band", "sub"),
        split_axis=0,
        concat_axis=0,
        tiled=True,
    ).reshape(-1, LANES)
    near_mates, near_crosses = across_bands(near_arrived)
    pre, mesh_place = local_call(
        edge_start_kernel,
        (shape(mesh_edges, latent), shape(mesh_edges, LANES, dtype=f32)),
        [whole()] * 3 + [in_hbm()] * 2,
        scratch=[
            pltpu.VMEM((mesh_edges, latent), bf16),
            pltpu.VMEM((latent, latent), bf16),
            pltpu.VMEM((mesh_edges, latent), bf16),
            pltpu.VMEM((mesh_edges, LANES), f32),
            pltpu.SemaphoreType.DMA((blocks + 1,)),
            pltpu.SemaphoreType.DMA((2 * blocks,)),
        ],
        flops=START_FLOPS,
        nbytes=START_BYTES,
        out_specs=(in_hbm(), in_hbm()),
        vmem=VMEM_ALL,
    )(mesh_src, mesh_dst, pairs, mesh_edge_lat, edge_self)
    return local_call(
        edge_finish_kernel,
        shape(mesh_rows, latent),
        [whole()] * 4 + [in_hbm()] * 13,
        scratch=[
            pltpu.VMEM((others, latent), bf16),
            pltpu.VMEM((far_total * latent // LANES, LANES), f32),
            pltpu.VMEM((mesh_edges, latent), bf16),
            pltpu.VMEM((mesh_edges, latent), bf16),
            pltpu.VMEM((mesh_edges, LANES), f32),
            pltpu.VMEM((mesh_edges, latent), bf16),
            pltpu.VMEM((4, latent, latent), bf16),
            pltpu.SemaphoreType.DMA((4,)),
            pltpu.SemaphoreType.DMA((3 * sub_count,)),
            pltpu.SemaphoreType.DMA((3 * blocks,)),
        ],
        flops=2 * mesh_edges * 2048 * latent,
        nbytes=12 << 20,
        vmem=VMEM_ALL,
    )(
        mesh_dst,
        far_rows,
        mesh_latent,
        out_gain.reshape(1, latent),
        pre,
        mesh_place,
        mesh_edge_lat,
        *near_arrived,
        near_mates,
        near_crosses,
        edge_out,
        upd_self,
        upd_agg,
        upd_out,
    )


def solution(mesh):
    rows = P(("band", "sub"), None)
    blocks = P(("band", "sub"), None, None)
    flat = P(("band", "sub"))
    return jax.shard_map(
        body,
        mesh=mesh,
        in_specs=(
            rows,
            blocks,
            flat,
            flat,
            flat,
            P(None, ("band", "sub")),
            rows,
            blocks,
            rows,
            flat,
            flat,
            rows,
        )
        + (P(),) * 18,
        out_specs=rows,
        check_vma=False,
    )
```

```python
import functools

import jax
import jax.numpy as jnp
from jax import lax
from jax.experimental import pallas as pl
from jax.experimental.pallas import tpu as pltpu
from jax.sharding import PartitionSpec as P

LANES = 128
EDGE_BLOCK = 512
PAIR = 2 * EDGE_BLOCK
VMEM_BYTES = 24 * 1024 * 1024
VMEM_ALL = 60 * 1024 * 1024
START_FLOPS = 4 * 10**9
START_BYTES = 16 << 20


def sub_swap(value, step):
    count = lax.axis_size("sub")
    return lax.ppermute(value, "sub", [(t, t ^ step) for t in range(count)])


def mate(band):
    return band ^ 1


def cross(band):
    return ((band + 1) ^ 1) - 1


def band_swap(value, partner):
    count = lax.axis_size("band")
    pairs = [(b, partner(b)) for b in range(count)]
    return lax.ppermute(value, "band", [(b, other) for b, other in pairs if 0 <= other < count])


def offsets():
    even = lax.rem(lax.axis_index("band"), 2) == 0
    return (1, jnp.where(even, 2, 0), jnp.where(even, 0, 2))


def sources():
    even = lax.rem(lax.axis_index("band"), 2) == 0
    return (1, jnp.where(even, 0, 2), jnp.where(even, 2, 0))


def layer_norm(values):
    row_mean = jnp.mean(values, axis=-1, keepdims=True)
    centred = values - row_mean
    variance = jnp.mean(centred * centred, axis=-1, keepdims=True)
    return centred * lax.rsqrt(variance + 1e-05)


def silu(values):
    half = 0.5 * values
    return half + half * jnp.tanh(half)


def dot(left, right):
    return jnp.dot(left, right, preferred_element_type=jnp.float32)


def half(values):
    return values.astype(jnp.bfloat16)


def column(row):
    return jnp.broadcast_to(row, (LANES, LANES)).T


def row_of(ref, first, count):
    return jnp.concatenate([ref[pl.ds(first + k, 1), :] for k in range(count)], axis=1)


def spread(rows, places):
    lanes = sum(1 for _ in places) * LANES
    lane = lax.broadcasted_iota(jnp.int32, (8, lanes), 1)
    row = lax.broadcasted_iota(jnp.int32, (8, lanes), 0)
    factors = jnp.zeros((8, lanes), jnp.float32)
    for k, entries in enumerate(places):
        for index, low, high, factor in entries:
            here = (row == index) & (lane >= k * LANES + low) & (lane < k * LANES + high)
            factors = jnp.where(here, factor, factors)
    return dot(half(rows.T), half(factors))


def digits(row):
    return [(row >> 7).astype(jnp.float32), (row & (LANES - 1)).astype(jnp.float32)]


def index_entry(first):
    return [(first, 0, LANES, float(LANES)), (first + 1, 0, LANES, 1.0)]


def lanes_of(indices):
    return lax.broadcasted_iota(jnp.int32, indices.shape, 1).astype(jnp.float32)


def picks(indices, width):
    lane = lanes_of(indices)
    indices = indices.astype(jnp.float32)
    parts = [
        half(jnp.where(indices == lane + float(first), 1.0, 0.0))
        for first in range(0, width, LANES)
    ]
    return jnp.concatenate(parts, axis=1)


def scatter_picks(row, height):
    shape = (height, row.shape[1])
    sub = lax.broadcasted_iota(jnp.int32, shape, 0)
    return half(jnp.where(sub == jnp.broadcast_to(row, shape), 1.0, 0.0))


def whole():
    return pl.BlockSpec(memory_space=pltpu.VMEM)


def in_smem():
    return pl.BlockSpec(memory_space=pltpu.SMEM)


def in_hbm():
    return pl.BlockSpec(memory_space=pltpu.HBM)


def local_call(
    kernel, out_shape, in_specs, scratch=(), flops=0, nbytes=0, out_specs=None, vmem=VMEM_BYTES
):
    return pl.pallas_call(
        kernel,
        out_shape=out_shape,
        in_specs=in_specs,
        out_specs=out_specs or jax.tree.map(lambda _: whole(), out_shape),
        scratch_shapes=list(scratch),
        compiler_params=pltpu.CompilerParams(vmem_limit_bytes=vmem),
        cost_estimate=pl.CostEstimate(flops=flops, bytes_accessed=nbytes, transcendentals=0),
    )


class Fetch:
    def __init__(self, refs, slots, sems):
        self.copies = [
            pltpu.make_async_copy(ref, slots.at[k], sems.at[k]) for k, ref in enumerate(refs)
        ]
        self.slots, self.ready = slots, set()
        for copy in self.copies:
            copy.start()

    def __call__(self, k):
        if k not in self.ready:
            self.copies[k].wait()
            self.ready.add(k)
        return self.slots.at[k]


def pick_grid_kernel(send_ref, grid_ref, *refs):
    out_refs, sum_ref = refs[:-1], refs[-1]
    width, rows = grid_ref.shape
    wide = out_refs[0].shape[-1]
    me = lax.axis_index("sub")
    part = pl.program_id(0)
    index = jnp.concatenate(
        [
            send_ref[offset, pl.ds(me ^ k, 1), :]
            for k in range(len(out_refs))
            for offset in offsets()
        ],
        axis=1,
    )
    picked = dot(grid_ref[...], scatter_picks(index - part * rows, rows))

    @pl.when(part == 0)
    def _():
        sum_ref[0:width, :] = picked
        sum_ref[width:, :] = jnp.zeros((wide - width, picked.shape[1]), jnp.float32)

    @pl.when(part > 0)
    def _():
        sum_ref[0:width, :] += picked

    @pl.when(part == pl.num_programs(0) - 1)
    def _():
        for k, out_ref in enumerate(out_refs):
            for w in range(3):
                first = (3 * k + w) * LANES
                out_ref[w] = half(sum_ref[:, first : first + LANES].T)


def prepare_grid_kernel(
    live_ref,
    src_ref,
    dst_ref,
    geo_ref,
    embed_ref,
    recv_proj_ref,
    geo_proj_ref,
    node_self_ref,
    place_ref,
    own_ref,
    node_ref,
    table_ref,
):
    mesh_rows, latent = embed_ref.shape
    base = table_ref.shape[0]
    geo_rows = geo_ref.shape[0]
    received = 3 * lax.axis_size("sub") * LANES
    is_last = lax.axis_index("band") == lax.axis_size("band") - 1
    src_shift = jnp.where(is_last, received // 3, 0)
    node_ref[...] = dot(embed_ref[...], node_self_ref[...])
    table_ref[0:mesh_rows, :] = half(dot(embed_ref[...], recv_proj_ref[...]))
    table_ref[mesh_rows:base, :] = half(
        jnp.concatenate(
            [
                geo_proj_ref[...].astype(jnp.float32),
                jnp.zeros((base - mesh_rows - geo_rows, latent), jnp.float32),
            ],
            axis=0,
        )
    )
    low = mesh_rows % LANES
    places = [
        index_entry(0),
        index_entry(2),
        [(4 + k, low + k, low + k + 1, 1.0) for k in range(geo_rows)],
    ]
    per = EDGE_BLOCK // LANES

    def step(block, carry):
        row0 = pl.multiple_of(block * EDGE_BLOCK, EDGE_BLOCK)
        rows = jnp.concatenate(
            digits(row_of(src_ref, block * per, per) - src_shift)
            + digits(row_of(dst_ref, block * per, per))
            + [geo_ref[:, pl.ds(row0, EDGE_BLOCK)].astype(jnp.float32)],
            axis=0,
        )
        wide = spread(rows, places)
        place_ref[pl.ds(row0, EDGE_BLOCK), :] = wide[:, 0:LANES]
        target = wide[:, LANES : 2 * LANES]
        lane = lanes_of(target)
        parts = []
        for k in range(base // LANES):
            part = jnp.where(target == lane + float(k * LANES), 1.0, 0.0)
            if k == mesh_rows // LANES:
                part = part + wide[:, 2 * LANES :]
            parts.append(half(part))
        own = dot(jnp.concatenate(parts, axis=1), table_ref[...])
        own_ref[pl.ds(row0, EDGE_BLOCK), :] = half(own)
        return carry

    lax.fori_loop(0, pl.cdiv(live_ref[0], PAIR) * (PAIR // EDGE_BLOCK), step, 0)


def encode_rows(rows, enc_in, enc_out, send_proj):
    hidden = half(silu(dot(rows, enc_in)))
    lat = half(layer_norm(dot(hidden, enc_out)))
    return half(dot(lat, send_proj))


def padded_rows(ref, rows):
    values = ref[...].astype(jnp.float32)
    zeros = jnp.zeros((rows - values.shape[0], values.shape[1]), jnp.float32)
    return half(jnp.concatenate([values, zeros], axis=0))


def encode_own_kernel(
    own0_ref, own1_ref, own2_ref, own3_ref, enc_in_ref, enc_out_ref, send_proj_ref, out_ref
):
    owns = (own0_ref, own1_ref, own2_ref, own3_ref)
    cap, wide = own0_ref.shape[1:]
    me = lax.axis_index("sub")
    sent = encode_rows(
        jnp.concatenate([ref[0] for ref in owns], axis=0),
        padded_rows(enc_in_ref, wide),
        enc_out_ref[...],
        send_proj_ref[...],
    )
    for k in range(len(owns)):
        out_ref[pl.ds(pl.multiple_of((me ^ k) * cap, cap), cap), :] = sent[
            k * cap : (k + 1) * cap
        ]


def encoder_kernel(
    live_ref,
    own_rows_ref,
    mate_ref,
    cross_ref,
    place_ref,
    own_ref,
    dst_ref,
    embed_ref,
    node_ref,
    near_ref,
    far_ref,
    enc_in_ref,
    gain_ref,
    enc_out_ref,
    send_proj_ref,
    msg_ref,
    node_agg_ref,
    node_out_ref,
    proc_send_ref,
    proc_recv_ref,
    latent_ref,
    pair_ref,
    out0_ref,
    out1_ref,
    out2_ref,
    out3_ref,
    out_far_ref,
    table_ref,
    sum_ref,
    flat_ref,
    act_ref,
    slots_ref,
    sems,
):
    weight = Fetch(
        (
            enc_out_ref,
            send_proj_ref,
            msg_ref,
            node_agg_ref,
            node_out_ref,
            proc_send_ref,
            proc_recv_ref,
        ),
        slots_ref,
        sems,
    )
    mesh_rows, latent = embed_ref.shape
    subs, cap, wide = mate_ref.shape
    chunk = subs * cap
    band, me = lax.axis_index("band"), lax.axis_index("sub")
    is_first = band == 0
    is_last = band == lax.axis_size("band") - 1
    polar = is_first | is_last
    live = live_ref[0]
    enc_in = padded_rows(enc_in_ref, wide)

    start = jnp.where(is_last, -chunk, 0)
    _, mate_place, cross_place = sources()
    table_ref[pl.ds(pl.multiple_of(start + chunk, chunk), chunk), :] = own_rows_ref[...]

    sent = encode_rows(
        jnp.concatenate([ref[...].reshape(chunk, wide) for ref in (mate_ref, cross_ref)], axis=0),
        enc_in,
        weight(0)[...],
        weight(1)[...],
    )
    firsts = (start + mate_place * chunk, jnp.where(polar, 2, cross_place) * chunk)
    for w, first in enumerate(firsts):
        for k in range(subs):
            place = pl.multiple_of(first + (me ^ k) * cap, cap)
            from_row = (w * subs + k) * cap
            table_ref[pl.ds(place, cap), :] = sent[from_row : from_row + cap]

    sum_ref[...] = jnp.zeros_like(sum_ref)

    def scatter(pair):
        lane = lax.broadcasted_iota(jnp.int32, (1, PAIR), 1)
        target = row_of(dst_ref, pair * (PAIR // LANES), PAIR // LANES)
        target = jnp.where(pair * PAIR + lane < live, target, -1)
        sum_ref[...] += dot(scatter_picks(target, mesh_rows), act_ref[...])

    act_ref[...] = half(
        silu(table_ref[0:PAIR, :].astype(jnp.float32) + own_ref[0:PAIR, :].astype(jnp.float32))
    )
    scatter(0)

    def edges(lookup_rows):
        def step(pair, carry):
            for k in range(PAIR // EDGE_BLOCK):
                row0 = pl.multiple_of(pair * PAIR + k * EDGE_BLOCK, EDGE_BLOCK)
                onehot = picks(place_ref[pl.ds(row0, EDGE_BLOCK), :], lookup_rows)
                pre = dot(onehot, table_ref[0:lookup_rows, :]) + own_ref[
                    pl.ds(row0, EDGE_BLOCK), :
                ].astype(jnp.float32)
                act_ref[k * EDGE_BLOCK : (k + 1) * EDGE_BLOCK, :] = half(silu(pre))
            scatter(pair)
            return carry

        lax.fori_loop(1, pl.cdiv(live, PAIR), step, 0)

    @pl.when(polar)
    def _():
        edges(2 * chunk)

    @pl.when(jnp.logical_not(polar))
    def _():
        edges(3 * chunk)

    total = sum_ref[...]
    high = half(total)
    low = half(total - high.astype(jnp.float32))
    both = dot(jnp.concatenate([high, low], axis=0), weight(2)[...])
    inflow = half(both[0:mesh_rows] + both[mesh_rows:])
    embed = embed_ref[...]
    node_act = half(silu(node_ref[...] + dot(inflow, weight(3)[...])))
    mesh_latent = half(
        embed.astype(jnp.float32) + layer_norm(dot(node_act, weight(4)[...])) * gain_ref[...]
    )
    latent_ref[...] = mesh_latent
    sender = half(dot(mesh_latent, weight(5)[...]))
    pair_ref[0:mesh_rows, :] = sender
    pair_ref[mesh_rows : 2 * mesh_rows, :] = half(dot(mesh_latent, weight(6)[...]))
    padded = -(-mesh_rows // LANES) * LANES
    sender_pad = jnp.concatenate(
        [sender, jnp.zeros((padded - mesh_rows, latent), jnp.bfloat16)], axis=0
    )
    near = near_ref.shape[2]
    shares = offsets()
    outs = (out0_ref, out1_ref, out2_ref, out3_ref)
    index = jnp.concatenate(
        [near_ref[offset, pl.ds(me ^ k, 1), :] for k in range(subs) for offset in shares]
        + [far_ref[c : c + 1, :] for c in range(far_ref.shape[0])],
        axis=1,
    )
    onehot = jnp.concatenate(
        [
            picks(column(index[:, first : first + LANES]), padded)
            for first in range(0, index.shape[1], LANES)
        ],
        axis=0,
    )
    leaving = dot(onehot, sender_pad)
    for k, out_ref in enumerate(outs):
        out_ref[...] = half(leaving[3 * near * k : 3 * near * (k + 1)]).reshape(out_ref.shape)
    lanes = latent // LANES
    spread_rows = far_ref.shape[0] * lanes
    for c in range(far_ref.shape[0]):
        first = 3 * near * subs + c * LANES
        for j in range(lanes):
            flat_ref[pl.ds(c * lanes + j, LANES, stride=spread_rows), :] = leaving[
                first : first + LANES, j * LANES : (j + 1) * LANES
            ]
    out_far_ref[...] = half(flat_ref[...])


def edge_start_kernel(
    src_ref,
    dst_ref,
    pair_hbm,
    lat_hbm,
    self_hbm,
    pre_hbm,
    place_hbm,
    pair_ref,
    lat_ref,
    self_ref,
    pre_ref,
    place_ref,
    read_sems,
    write_sems,
):
    mesh_rows = pair_ref.shape[0] // 2
    subs = lax.axis_size("sub")
    devices = lax.axis_size("band") * subs
    near_total = 3 * subs * (LANES // 2)
    edges = lat_ref.shape[0]
    halves = [pl.ds(first, edges // 2) for first in (0, edges // 2)]
    pairs = pltpu.make_async_copy(pair_hbm, pair_ref, read_sems.at[3])
    weight = pltpu.make_async_copy(self_hbm, self_ref, read_sems.at[2])
    reads = [
        pltpu.make_async_copy(lat_hbm.at[span], lat_ref.at[span], read_sems.at[k])
        for k, span in enumerate(halves)
    ]
    for copy in [pairs, weight, *reads]:
        copy.start()
    source = row_of(src_ref, 0, edges // LANES)
    target = row_of(dst_ref, 0, edges // LANES)
    other = source - mesh_rows
    far = other - near_total
    far = near_total + (far & 1) * devices + (far >> 1)
    rows = jnp.concatenate(
        digits(jnp.where(source < mesh_rows, source, -1))
        + digits(target + mesh_rows)
        + digits(jnp.where(other < near_total, other, far))
        + [jnp.zeros((2, edges), jnp.float32)],
        axis=0,
    )
    wide = spread(rows, [index_entry(0), index_entry(2), index_entry(4)])
    own, mine = wide[:, 0:LANES], wide[:, LANES : 2 * LANES]
    place_ref[...] = wide[:, 2 * LANES :]
    writes = [pltpu.make_async_copy(place_ref, place_hbm, write_sems.at[2])]
    writes[0].start()
    lane = lanes_of(own)
    parts = []
    for first in range(0, 2 * mesh_rows, LANES):
        hit = None
        if first < mesh_rows:
            hit = own == lane + float(first)
        if first + LANES > mesh_rows:
            match = mine == lane + float(first)
            hit = match if hit is None else hit | match
        parts.append(half(jnp.where(hit, 1.0, 0.0)))
    onehot = jnp.concatenate(parts, axis=1)
    pairs.wait()
    weight.wait()
    for k, span in enumerate(halves):
        picked = dot(onehot[k * (edges // 2) : (k + 1) * (edges // 2)], pair_ref[...])
        reads[k].wait()
        pre_ref[span, :] = half(picked + dot(lat_ref[span, :], self_ref[...]))
        writes.append(
            pltpu.make_async_copy(pre_ref.at[span], pre_hbm.at[span], write_sems.at[k])
        )
        writes[-1].start()
    for copy in writes:
        copy.wait()


def edge_finish_kernel(
    dst_ref,
    gain_ref,
    far_hbm,
    latent_hbm,
    pre_hbm,
    place_hbm,
    lat_hbm,
    own0_hbm,
    own1_hbm,
    own2_hbm,
    own3_hbm,
    mate_hbm,
    cross_hbm,
    edge_out_ref,
    upd_self_ref,
    upd_agg_ref,
    upd_out_ref,
    out_ref,
    far_ref,
    latent_ref,
    table_ref,
    flat_ref,
    new_ref,
    pre_ref,
    place_ref,
    lat_ref,
    slots_ref,
    sems,
    table_sems,
    block_sems,
):
    mesh_rows, latent = latent_ref.shape
    blocks = 2
    block_rows = lat_ref.shape[0] // blocks
    spans = [pl.ds(block * block_rows, block_rows) for block in range(blocks)]
    subs, near, _ = mate_hbm.shape
    near_total = 3 * subs * near
    me = lax.axis_index("sub")
    owns = (own0_hbm, own1_hbm, own2_hbm, own3_hbm)
    rows = []
    for w, offset in enumerate(sources()):
        for k in range(subs):
            source = owns[k].at[0] if w == 0 else (mate_hbm, cross_hbm)[w - 1].at[k]
            place = pl.multiple_of((offset * subs + (me ^ k)) * near, near)
            rows.append(
                pltpu.make_async_copy(
                    source, table_ref.at[pl.ds(place, near)], table_sems.at[w * subs + k]
                )
            )
    moved = ((pre_hbm, pre_ref), (place_hbm, place_ref), (lat_hbm, lat_ref))
    reads = [
        [
            pltpu.make_async_copy(hbm.at[span], ref.at[span], block_sems.at[3 * k + j])
            for j, (hbm, ref) in enumerate(moved)
        ]
        for k, span in enumerate(spans)
    ]
    far_read = pltpu.make_async_copy(far_hbm, far_ref, sems.at[4])
    latent_read = pltpu.make_async_copy(latent_hbm, latent_ref, sems.at[5])
    for copy in [far_read, *rows, reads[0][1], reads[0][0], latent_read]:
        copy.start()
    weight = Fetch((edge_out_ref, upd_self_ref, upd_agg_ref, upd_out_ref), slots_ref, sems)
    reads[0][2].start()
    for block in reads[1:]:
        for copy in block:
            copy.start()
    lanes = latent // LANES
    devices = far_ref.shape[0] // (2 * lanes)
    far_read.wait()
    flat_ref[...] = far_ref[...].astype(jnp.float32)
    for c in range(2):
        table_ref[pl.ds(near_total + c * devices, devices), :] = half(
            jnp.concatenate(
                [
                    flat_ref[pl.ds(c * lanes + j, devices, stride=2 * lanes), :]
                    for j in range(lanes)
                ],
                axis=1,
            )
        )
    for copy in rows:
        copy.wait()
    edge_out = weight(0)[...]
    latent_read.wait()
    upd_self = dot(latent_ref[...], weight(1)[...])

    def gathered(block):
        span = spans[block]
        for copy in reads[block]:
            copy.wait()
        return pre_ref[span, :].astype(jnp.float32) + dot(
            picks(place_ref[span, :], table_ref.shape[0]), table_ref[...]
        )

    def settle(block, pre):
        span = spans[block]
        out = layer_norm(dot(half(silu(pre)), edge_out))
        new_ref[span, :] = half(lat_ref[span, :].astype(jnp.float32) + out)

    pre = gathered(0)
    for block in range(1, blocks):
        later = gathered(block)
        settle(block - 1, pre)
        pre = later
    settle(blocks - 1, pre)
    target = row_of(dst_ref, 0, lat_ref.shape[0] // LANES)
    inflow = half(dot(scatter_picks(target, mesh_rows), new_ref[...]))
    latent = latent_ref[...]
    act = half(silu(upd_self + dot(inflow, weight(2)[...])))
    out_ref[...] = half(
        latent.astype(jnp.float32) + layer_norm(dot(act, weight(3)[...])) * gain_ref[...]
    )


def body(
    grid_input,
    grid_send,
    grid_edge_src,
    grid_edge_dst,
    edge_count,
    grid_edge_geo,
    mesh_embed,
    mesh_near_send,
    mesh_far_send,
    mesh_edge_src,
    mesh_edge_dst,
    mesh_edge_lat,
    enc_in,
    enc_out,
    send_proj,
    recv_proj,
    geo_proj,
    msg_weight,
    node_self,
    node_agg,
    node_out,
    mesh_gain,
    proc_send,
    proc_recv,
    edge_self,
    edge_out,
    upd_self,
    upd_agg,
    upd_out,
    out_gain,
):
    sub_count = lax.axis_size("sub")
    devices = lax.axis_size("band") * sub_count
    slot_cap = grid_send.shape[2]
    near_cap = mesh_near_send.shape[2]
    far_cap = mesh_far_send.shape[1]
    mesh_rows, latent = mesh_embed.shape
    edges = grid_edge_src.shape[0]
    mesh_edges = mesh_edge_src.shape[0]
    wide = 256
    bf16, f32 = jnp.bfloat16, jnp.float32

    def across_subs(parts):
        return [parts[0]] + [sub_swap(parts[k], k) for k in range(1, sub_count)]

    def across_bands(arrived):
        mates = band_swap(jnp.stack([part[1] for part in arrived]), mate)
        crosses = band_swap(jnp.stack([part[2] for part in arrived]), cross)
        return mates, crosses

    def shape(*dims, dtype=bf16):
        return jax.ShapeDtypeStruct(dims, dtype)

    received = sub_count * slot_cap
    halves = grid_input.shape[0] // 2
    parts = pl.pallas_call(
        pick_grid_kernel,
        grid=(2,),
        out_shape=(shape(3, slot_cap, wide),) * sub_count,
        in_specs=[
            pl.BlockSpec(grid_send.shape, lambda i: (0, 0, 0)),
            pl.BlockSpec((grid_input.shape[1], halves), lambda i: (0, i)),
        ],
        out_specs=(pl.BlockSpec((3, slot_cap, wide), lambda i: (0, 0, 0)),) * sub_count,
        scratch_shapes=[pltpu.VMEM((wide, 3 * received), f32)],
        compiler_params=pltpu.CompilerParams(vmem_limit_bytes=VMEM_ALL),
        cost_estimate=pl.CostEstimate(
            flops=6 * received * grid_input.shape[0] * wide,
            bytes_accessed=2 * wide * (3 * received + grid_input.shape[0]),
            transcendentals=0,
        ),
    )(grid_send, grid_input.T)
    arrived = across_subs(parts)

    far_total = devices * far_cap
    others = 3 * sub_count * near_cap + far_total
    blocks = mesh_edges // EDGE_BLOCK
    edge_src, _ = lax.optimization_barrier((grid_edge_src, parts[0]))
    edge_dst = grid_edge_dst.reshape(-1, LANES)
    mesh_src = mesh_edge_src.reshape(-1, LANES)
    mesh_dst = mesh_edge_dst.reshape(-1, LANES)
    place, own, node = local_call(
        prepare_grid_kernel,
        (
            shape(edges, LANES, dtype=f32),
            shape(edges, latent),
            shape(mesh_rows, latent, dtype=f32),
        ),
        [in_smem()] + [whole()] * 7,
        scratch=[pltpu.VMEM((384, latent), bf16)],
        flops=2 * edges * 1024 * latent,
        nbytes=16 << 20,
    )(
        edge_count,
        edge_src.reshape(-1, LANES),
        edge_dst,
        grid_edge_geo,
        mesh_embed,
        recv_proj,
        geo_proj,
        node_self,
    )

    arrived, place, own, node = lax.optimization_barrier((arrived, place, own, node))
    mates, crosses = across_bands(arrived)
    own_rows = local_call(
        encode_own_kernel,
        shape(received, latent),
        [whole()] * 7,
        flops=2 * received * 1280 * latent,
        nbytes=3 << 20,
    )(*arrived, enc_in, enc_out, send_proj)

    mesh_latent, pairs, *near_parts, far_out = local_call(
        encoder_kernel,
        (
            shape(mesh_rows, latent),
            shape(2 * mesh_rows, latent),
        )
        + (shape(3, near_cap, latent),) * sub_count
        + (shape(far_total * latent // LANES, LANES),),
        [in_smem()] + [whole()] * 12 + [in_hbm()] * 7,
        scratch=[
            pltpu.VMEM((3 * received, latent), bf16),
            pltpu.VMEM((mesh_rows, latent), f32),
            pltpu.VMEM((far_total * latent // LANES, LANES), f32),
            pltpu.VMEM((PAIR, latent), bf16),
            pltpu.VMEM((7, latent, latent), bf16),
            pltpu.SemaphoreType.DMA((7,)),
        ],
        flops=2 * edges * 2048 * latent,
        nbytes=16 << 20,
    )(
        edge_count,
        own_rows,
        mates,
        crosses,
        place,
        own,
        edge_dst,
        mesh_embed,
        node,
        mesh_near_send,
        mesh_far_send.T,
        enc_in,
        mesh_gain.reshape(1, latent),
        enc_out,
        send_proj,
        msg_weight,
        node_agg,
        node_out,
        proc_send,
        proc_recv,
    )

    near_arrived = across_subs(near_parts)
    near_arrived[1], far_out = lax.optimization_barrier((near_arrived[1], far_out))
    far_rows = lax.all_to_all(
        far_out.reshape(devices, -1, LANES),
        ("band", "sub"),
        split_axis=0,
        concat_axis=0,
        tiled=True,
    ).reshape(-1, LANES)
    near_mates, near_crosses = across_bands(near_arrived)
    pre, mesh_place = local_call(
        edge_start_kernel,
        (shape(mesh_edges, latent), shape(mesh_edges, LANES, dtype=f32)),
        [whole()] * 2 + [in_hbm()] * 3,
        scratch=[
            pltpu.VMEM((2 * mesh_rows, latent), bf16),
            pltpu.VMEM((mesh_edges, latent), bf16),
            pltpu.VMEM((latent, latent), bf16),
            pltpu.VMEM((mesh_edges, latent), bf16),
            pltpu.VMEM((mesh_edges, LANES), f32),
            pltpu.SemaphoreType.DMA((4,)),
            pltpu.SemaphoreType.DMA((3,)),
        ],
        flops=START_FLOPS,
        nbytes=START_BYTES,
        out_specs=(in_hbm(), in_hbm()),
        vmem=VMEM_ALL,
    )(mesh_src, mesh_dst, pairs, mesh_edge_lat, edge_self)
    return local_call(
        edge_finish_kernel,
        shape(mesh_rows, latent),
        [whole()] * 2 + [in_hbm()] * 15,
        scratch=[
            pltpu.VMEM(far_rows.shape, bf16),
            pltpu.VMEM((mesh_rows, latent), bf16),
            pltpu.VMEM((others, latent), bf16),
            pltpu.VMEM((far_total * latent // LANES, LANES), f32),
            pltpu.VMEM((mesh_edges, latent), bf16),
            pltpu.VMEM((mesh_edges, latent), bf16),
            pltpu.VMEM((mesh_edges, LANES), f32),
            pltpu.VMEM((mesh_edges, latent), bf16),
            pltpu.VMEM((4, latent, latent), bf16),
            pltpu.SemaphoreType.DMA((6,)),
            pltpu.SemaphoreType.DMA((3 * sub_count,)),
            pltpu.SemaphoreType.DMA((3 * blocks,)),
        ],
        flops=2 * mesh_edges * 2048 * latent,
        nbytes=12 << 20,
        vmem=VMEM_ALL,
    )(
        mesh_dst,
        out_gain.reshape(1, latent),
        far_rows,
        mesh_latent,
        pre,
        mesh_place,
        mesh_edge_lat,
        *near_arrived,
        near_mates,
        near_crosses,
        edge_out,
        upd_self,
        upd_agg,
        upd_out,
    )


def solution(mesh):
    rows = P(("band", "sub"), None)
    blocks = P(("band", "sub"), None, None)
    flat = P(("band", "sub"))
    return jax.shard_map(
        body,
        mesh=mesh,
        in_specs=(
            rows,
            blocks,
            flat,
            flat,
            flat,
            P(None, ("band", "sub")),
            rows,
            blocks,
            rows,
            flat,
            flat,
            rows,
        )
        + (P(),) * 18,
        out_specs=rows,
        check_vma=False,
    )
```

```python
import functools

import jax
import jax.numpy as jnp
from jax import lax
from jax.experimental import pallas as pl
from jax.experimental.pallas import tpu as pltpu
from jax.sharding import PartitionSpec as P

LANES = 128
EDGE_BLOCK = 512
PAIR = 2 * EDGE_BLOCK
VMEM_BYTES = 24 * 1024 * 1024
VMEM_ALL = 60 * 1024 * 1024
START_FLOPS = 4 * 10**9
START_BYTES = 16 << 20


def sub_swap(value, step):
    count = lax.axis_size("sub")
    return lax.ppermute(value, "sub", [(t, t ^ step) for t in range(count)])


def mate(band):
    return band ^ 1


def cross(band):
    return ((band + 1) ^ 1) - 1


def band_swap(value, partner):
    count = lax.axis_size("band")
    pairs = [(b, partner(b)) for b in range(count)]
    return lax.ppermute(value, "band", [(b, other) for b, other in pairs if 0 <= other < count])


def offsets():
    even = lax.rem(lax.axis_index("band"), 2) == 0
    return (1, jnp.where(even, 2, 0), jnp.where(even, 0, 2))


def sources():
    even = lax.rem(lax.axis_index("band"), 2) == 0
    return (1, jnp.where(even, 0, 2), jnp.where(even, 2, 0))


def layer_norm(values):
    row_mean = jnp.mean(values, axis=-1, keepdims=True)
    centred = values - row_mean
    variance = jnp.mean(centred * centred, axis=-1, keepdims=True)
    return centred * lax.rsqrt(variance + 1e-05)


def silu(values):
    half = 0.5 * values
    return half + half * jnp.tanh(half)


def dot(left, right):
    return jnp.dot(left, right, preferred_element_type=jnp.float32)


def half(values):
    return values.astype(jnp.bfloat16)


def column(row):
    return jnp.broadcast_to(row, (LANES, LANES)).T


def row_of(ref, first, count):
    return jnp.concatenate([ref[pl.ds(first + k, 1), :] for k in range(count)], axis=1)


def spread(rows, places):
    lanes = sum(1 for _ in places) * LANES
    lane = lax.broadcasted_iota(jnp.int32, (8, lanes), 1)
    row = lax.broadcasted_iota(jnp.int32, (8, lanes), 0)
    factors = jnp.zeros((8, lanes), jnp.float32)
    for k, entries in enumerate(places):
        for index, low, high, factor in entries:
            here = (row == index) & (lane >= k * LANES + low) & (lane < k * LANES + high)
            factors = jnp.where(here, factor, factors)
    return dot(half(rows.T), half(factors))


def digits(row):
    return [(row >> 7).astype(jnp.float32), (row & (LANES - 1)).astype(jnp.float32)]


def index_entry(first):
    return [(first, 0, LANES, float(LANES)), (first + 1, 0, LANES, 1.0)]


def lanes_of(indices):
    return lax.broadcasted_iota(jnp.int32, indices.shape, 1).astype(jnp.float32)


def picks(indices, width):
    lane = lanes_of(indices)
    indices = indices.astype(jnp.float32)
    parts = [
        half(jnp.where(indices == lane + float(first), 1.0, 0.0))
        for first in range(0, width, LANES)
    ]
    return jnp.concatenate(parts, axis=1)


def scatter_picks(row, height):
    shape = (height, row.shape[1])
    sub = lax.broadcasted_iota(jnp.int32, shape, 0)
    return half(jnp.where(sub == jnp.broadcast_to(row, shape), 1.0, 0.0))


def whole():
    return pl.BlockSpec(memory_space=pltpu.VMEM)


def in_smem():
    return pl.BlockSpec(memory_space=pltpu.SMEM)


def in_hbm():
    return pl.BlockSpec(memory_space=pltpu.HBM)


def local_call(
    kernel, out_shape, in_specs, scratch=(), flops=0, nbytes=0, out_specs=None, vmem=VMEM_BYTES
):
    return pl.pallas_call(
        kernel,
        out_shape=out_shape,
        in_specs=in_specs,
        out_specs=out_specs or jax.tree.map(lambda _: whole(), out_shape),
        scratch_shapes=list(scratch),
        compiler_params=pltpu.CompilerParams(vmem_limit_bytes=vmem),
        cost_estimate=pl.CostEstimate(flops=flops, bytes_accessed=nbytes, transcendentals=0),
    )


class Fetch:
    def __init__(self, refs, slots, sems):
        self.copies = [
            pltpu.make_async_copy(ref, slots.at[k], sems.at[k]) for k, ref in enumerate(refs)
        ]
        self.slots, self.ready = slots, set()
        for copy in self.copies:
            copy.start()

    def __call__(self, k):
        if k not in self.ready:
            self.copies[k].wait()
            self.ready.add(k)
        return self.slots.at[k]


def pick_grid_kernel(send_ref, grid_ref, *refs):
    out_refs, sum_ref = refs[:-1], refs[-1]
    width, rows = grid_ref.shape
    wide = out_refs[0].shape[-1]
    me = lax.axis_index("sub")
    part = pl.program_id(0)
    index = jnp.concatenate(
        [
            send_ref[offset, pl.ds(me ^ k, 1), :]
            for k in range(len(out_refs))
            for offset in offsets()
        ],
        axis=1,
    )
    picked = dot(grid_ref[...], scatter_picks(index - part * rows, rows))

    @pl.when(part == 0)
    def _():
        sum_ref[0:width, :] = picked
        sum_ref[width:, :] = jnp.zeros((wide - width, picked.shape[1]), jnp.float32)

    @pl.when(part > 0)
    def _():
        sum_ref[0:width, :] += picked

    @pl.when(part == pl.num_programs(0) - 1)
    def _():
        for k, out_ref in enumerate(out_refs):
            for w in range(3):
                first = (3 * k + w) * LANES
                out_ref[w] = half(sum_ref[:, first : first + LANES].T)


def prepare_grid_kernel(
    live_ref,
    src_ref,
    dst_ref,
    geo_ref,
    embed_ref,
    recv_proj_ref,
    geo_proj_ref,
    node_self_ref,
    place_ref,
    own_ref,
    node_ref,
    table_ref,
):
    mesh_rows, latent = embed_ref.shape
    base = table_ref.shape[0]
    geo_rows = geo_ref.shape[0]
    received = 3 * lax.axis_size("sub") * LANES
    is_last = lax.axis_index("band") == lax.axis_size("band") - 1
    src_shift = jnp.where(is_last, received // 3, 0)
    node_ref[...] = dot(embed_ref[...], node_self_ref[...])
    table_ref[0:mesh_rows, :] = half(dot(embed_ref[...], recv_proj_ref[...]))
    table_ref[mesh_rows:base, :] = half(
        jnp.concatenate(
            [
                geo_proj_ref[...].astype(jnp.float32),
                jnp.zeros((base - mesh_rows - geo_rows, latent), jnp.float32),
            ],
            axis=0,
        )
    )
    low = mesh_rows % LANES
    places = [
        index_entry(0),
        index_entry(2),
        [(4 + k, low + k, low + k + 1, 1.0) for k in range(geo_rows)],
    ]
    per = EDGE_BLOCK // LANES

    def step(block, carry):
        row0 = pl.multiple_of(block * EDGE_BLOCK, EDGE_BLOCK)
        rows = jnp.concatenate(
            digits(row_of(src_ref, block * per, per) - src_shift)
            + digits(row_of(dst_ref, block * per, per))
            + [geo_ref[:, pl.ds(row0, EDGE_BLOCK)].astype(jnp.float32)],
            axis=0,
        )
        wide = spread(rows, places)
        place_ref[pl.ds(row0, EDGE_BLOCK), :] = wide[:, 0:LANES]
        target = wide[:, LANES : 2 * LANES]
        lane = lanes_of(target)
        parts = []
        for k in range(base // LANES):
            part = jnp.where(target == lane + float(k * LANES), 1.0, 0.0)
            if k == mesh_rows // LANES:
                part = part + wide[:, 2 * LANES :]
            parts.append(half(part))
        own = dot(jnp.concatenate(parts, axis=1), table_ref[...])
        own_ref[pl.ds(row0, EDGE_BLOCK), :] = half(own)
        return carry

    lax.fori_loop(0, pl.cdiv(live_ref[0], PAIR) * (PAIR // EDGE_BLOCK), step, 0)


def encode_rows(rows, enc_in, enc_out, send_proj):
    hidden = half(silu(dot(rows, enc_in)))
    lat = half(layer_norm(dot(hidden, enc_out)))
    return half(dot(lat, send_proj))


def padded_rows(ref, rows):
    values = ref[...].astype(jnp.float32)
    zeros = jnp.zeros((rows - values.shape[0], values.shape[1]), jnp.float32)
    return half(jnp.concatenate([values, zeros], axis=0))


def encode_own_kernel(
    own0_ref, own1_ref, own2_ref, own3_ref, enc_in_ref, enc_out_ref, send_proj_ref, out_ref
):
    owns = (own0_ref, own1_ref, own2_ref, own3_ref)
    cap, wide = own0_ref.shape[1:]
    me = lax.axis_index("sub")
    sent = encode_rows(
        jnp.concatenate([ref[0] for ref in owns], axis=0),
        padded_rows(enc_in_ref, wide),
        enc_out_ref[...],
        send_proj_ref[...],
    )
    for k in range(len(owns)):
        out_ref[pl.ds(pl.multiple_of((me ^ k) * cap, cap), cap), :] = sent[
            k * cap : (k + 1) * cap
        ]


def encoder_kernel(
    live_ref,
    own_rows_ref,
    mate_ref,
    cross_ref,
    place_ref,
    own_ref,
    dst_ref,
    embed_ref,
    node_ref,
    near_ref,
    far_ref,
    enc_in_ref,
    gain_ref,
    enc_out_ref,
    send_proj_ref,
    msg_ref,
    node_agg_ref,
    node_out_ref,
    proc_send_ref,
    proc_recv_ref,
    trio_ref,
    out1_ref,
    out2_ref,
    out3_ref,
    out_far_ref,
    table_ref,
    sum_ref,
    flat_ref,
    act_ref,
    slots_ref,
    sems,
):
    weight = Fetch(
        (
            enc_out_ref,
            send_proj_ref,
            msg_ref,
            node_agg_ref,
            node_out_ref,
            proc_send_ref,
            proc_recv_ref,
        ),
        slots_ref,
        sems,
    )
    mesh_rows, latent = embed_ref.shape
    subs, cap, wide = mate_ref.shape
    chunk = subs * cap
    band, me = lax.axis_index("band"), lax.axis_index("sub")
    is_first = band == 0
    is_last = band == lax.axis_size("band") - 1
    polar = is_first | is_last
    live = live_ref[0]
    enc_in = padded_rows(enc_in_ref, wide)

    start = jnp.where(is_last, -chunk, 0)
    _, mate_place, cross_place = sources()
    table_ref[pl.ds(pl.multiple_of(start + chunk, chunk), chunk), :] = own_rows_ref[...]

    sent = encode_rows(
        jnp.concatenate([ref[...].reshape(chunk, wide) for ref in (mate_ref, cross_ref)], axis=0),
        enc_in,
        weight(0)[...],
        weight(1)[...],
    )
    firsts = (start + mate_place * chunk, jnp.where(polar, 2, cross_place) * chunk)
    for w, first in enumerate(firsts):
        for k in range(subs):
            place = pl.multiple_of(first + (me ^ k) * cap, cap)
            from_row = (w * subs + k) * cap
            table_ref[pl.ds(place, cap), :] = sent[from_row : from_row + cap]

    sum_ref[...] = jnp.zeros_like(sum_ref)

    def scatter(pair):
        lane = lax.broadcasted_iota(jnp.int32, (1, PAIR), 1)
        target = row_of(dst_ref, pair * (PAIR // LANES), PAIR // LANES)
        target = jnp.where(pair * PAIR + lane < live, target, -1)
        sum_ref[...] += dot(scatter_picks(target, mesh_rows), act_ref[...])

    act_ref[...] = half(
        silu(table_ref[0:PAIR, :].astype(jnp.float32) + own_ref[0:PAIR, :].astype(jnp.float32))
    )
    scatter(0)

    def edges(lookup_rows):
        def step(pair, carry):
            for k in range(PAIR // EDGE_BLOCK):
                row0 = pl.multiple_of(pair * PAIR + k * EDGE_BLOCK, EDGE_BLOCK)
                onehot = picks(place_ref[pl.ds(row0, EDGE_BLOCK), :], lookup_rows)
                pre = dot(onehot, table_ref[0:lookup_rows, :]) + own_ref[
                    pl.ds(row0, EDGE_BLOCK), :
                ].astype(jnp.float32)
                act_ref[k * EDGE_BLOCK : (k + 1) * EDGE_BLOCK, :] = half(silu(pre))
            scatter(pair)
            return carry

        lax.fori_loop(1, pl.cdiv(live, PAIR), step, 0)

    @pl.when(polar)
    def _():
        edges(2 * chunk)

    @pl.when(jnp.logical_not(polar))
    def _():
        edges(3 * chunk)

    total = sum_ref[...]
    high = half(total)
    low = half(total - high.astype(jnp.float32))
    both = dot(jnp.concatenate([high, low], axis=0), weight(2)[...])
    inflow = half(both[0:mesh_rows] + both[mesh_rows:])
    embed = embed_ref[...]
    node_act = half(silu(node_ref[...] + dot(inflow, weight(3)[...])))
    mesh_latent = half(
        embed.astype(jnp.float32) + layer_norm(dot(node_act, weight(4)[...])) * gain_ref[...]
    )
    trio_ref[2 * mesh_rows : 3 * mesh_rows, :] = mesh_latent
    sender = half(dot(mesh_latent, weight(5)[...]))
    trio_ref[0:mesh_rows, :] = sender
    trio_ref[mesh_rows : 2 * mesh_rows, :] = half(dot(mesh_latent, weight(6)[...]))
    padded = -(-mesh_rows // LANES) * LANES
    sender_pad = jnp.concatenate(
        [sender, jnp.zeros((padded - mesh_rows, latent), jnp.bfloat16)], axis=0
    )
    near = near_ref.shape[2]
    shares = offsets()
    outs = (out1_ref, out2_ref, out3_ref)
    index = jnp.concatenate(
        [near_ref[offset, pl.ds(me ^ k, 1), :] for k in range(subs) for offset in shares]
        + [far_ref[c : c + 1, :] for c in range(far_ref.shape[0])],
        axis=1,
    )
    onehot = jnp.concatenate(
        [
            picks(column(index[:, first : first + LANES]), padded)
            for first in range(0, index.shape[1], LANES)
        ],
        axis=0,
    )
    leaving = dot(onehot, sender_pad)
    trio_ref[3 * mesh_rows :, :] = half(leaving[0 : 3 * near])
    for k, out_ref in enumerate(outs, 1):
        out_ref[...] = half(leaving[3 * near * k : 3 * near * (k + 1)]).reshape(out_ref.shape)
    lanes = latent // LANES
    spread_rows = far_ref.shape[0] * lanes
    for c in range(far_ref.shape[0]):
        first = 3 * near * subs + c * LANES
        for j in range(lanes):
            flat_ref[pl.ds(c * lanes + j, LANES, stride=spread_rows), :] = leaving[
                first : first + LANES, j * LANES : (j + 1) * LANES
            ]
    out_far_ref[...] = half(flat_ref[...])


def edge_start_kernel(
    src_ref,
    dst_ref,
    trio_hbm,
    lat_hbm,
    self_hbm,
    pre_hbm,
    place_hbm,
    pair_ref,
    lat_ref,
    self_ref,
    pre_ref,
    place_ref,
    read_sems,
    write_sems,
):
    mesh_rows = pair_ref.shape[0] // 2
    subs = lax.axis_size("sub")
    devices = lax.axis_size("band") * subs
    near_total = 3 * subs * (LANES // 2)
    edges = lat_ref.shape[0]
    halves = [pl.ds(first, edges // 2) for first in (0, edges // 2)]
    pairs = pltpu.make_async_copy(
        trio_hbm.at[pl.ds(0, pair_ref.shape[0])], pair_ref, read_sems.at[3]
    )
    weight = pltpu.make_async_copy(self_hbm, self_ref, read_sems.at[2])
    reads = [
        pltpu.make_async_copy(lat_hbm.at[span], lat_ref.at[span], read_sems.at[k])
        for k, span in enumerate(halves)
    ]
    for copy in [pairs, weight, *reads]:
        copy.start()
    source = row_of(src_ref, 0, edges // LANES)
    target = row_of(dst_ref, 0, edges // LANES)
    other = source - mesh_rows
    far = other - near_total
    far = near_total + (far & 1) * devices + (far >> 1)
    rows = jnp.concatenate(
        digits(jnp.where(source < mesh_rows, source, -1))
        + digits(target + mesh_rows)
        + digits(jnp.where(other < near_total, other, far))
        + [jnp.zeros((2, edges), jnp.float32)],
        axis=0,
    )
    wide = spread(rows, [index_entry(0), index_entry(2), index_entry(4)])
    own, mine = wide[:, 0:LANES], wide[:, LANES : 2 * LANES]
    place_ref[...] = wide[:, 2 * LANES :]
    writes = [pltpu.make_async_copy(place_ref, place_hbm, write_sems.at[2])]
    writes[0].start()
    lane = lanes_of(own)
    parts = []
    for first in range(0, 2 * mesh_rows, LANES):
        hit = None
        if first < mesh_rows:
            hit = own == lane + float(first)
        if first + LANES > mesh_rows:
            match = mine == lane + float(first)
            hit = match if hit is None else hit | match
        parts.append(half(jnp.where(hit, 1.0, 0.0)))
    onehot = jnp.concatenate(parts, axis=1)
    pairs.wait()
    weight.wait()
    for k, span in enumerate(halves):
        picked = dot(onehot[k * (edges // 2) : (k + 1) * (edges // 2)], pair_ref[...])
        reads[k].wait()
        pre_ref[span, :] = half(picked + dot(lat_ref[span, :], self_ref[...]))
        writes.append(
            pltpu.make_async_copy(pre_ref.at[span], pre_hbm.at[span], write_sems.at[k])
        )
        writes[-1].start()
    for copy in writes:
        copy.wait()


def edge_finish_kernel(
    dst_ref,
    gain_ref,
    far_hbm,
    trio_hbm,
    pre_hbm,
    place_hbm,
    lat_hbm,
    own1_hbm,
    own2_hbm,
    own3_hbm,
    mate_hbm,
    cross_hbm,
    edge_out_ref,
    upd_self_ref,
    upd_agg_ref,
    upd_out_ref,
    out_ref,
    far_ref,
    latent_ref,
    table_ref,
    flat_ref,
    new_ref,
    pre_ref,
    place_ref,
    lat_ref,
    slots_ref,
    sems,
    table_sems,
    block_sems,
):
    mesh_rows, latent = latent_ref.shape
    blocks = 2
    block_rows = lat_ref.shape[0] // blocks
    spans = [pl.ds(block * block_rows, block_rows) for block in range(blocks)]
    subs, near, _ = mate_hbm.shape
    near_total = 3 * subs * near
    me = lax.axis_index("sub")
    owns = (trio_hbm, own1_hbm, own2_hbm, own3_hbm)
    stay = pl.ds(3 * latent_ref.shape[0], mate_hbm.shape[1])
    rows = []
    for w, offset in enumerate(sources()):
        for k in range(subs):
            own = owns[k].at[stay] if k == 0 else owns[k].at[0]
            source = own if w == 0 else (mate_hbm, cross_hbm)[w - 1].at[k]
            place = pl.multiple_of((offset * subs + (me ^ k)) * near, near)
            rows.append(
                pltpu.make_async_copy(
                    source, table_ref.at[pl.ds(place, near)], table_sems.at[w * subs + k]
                )
            )
    moved = ((pre_hbm, pre_ref), (place_hbm, place_ref), (lat_hbm, lat_ref))
    reads = [
        [
            pltpu.make_async_copy(hbm.at[span], ref.at[span], block_sems.at[3 * k + j])
            for j, (hbm, ref) in enumerate(moved)
        ]
        for k, span in enumerate(spans)
    ]
    far_read = pltpu.make_async_copy(far_hbm, far_ref, sems.at[4])
    latent_read = pltpu.make_async_copy(
        trio_hbm.at[pl.ds(2 * mesh_rows, mesh_rows)], latent_ref, sems.at[5]
    )
    for copy in [far_read, *rows, reads[0][1], reads[0][0], latent_read]:
        copy.start()
    weight = Fetch((edge_out_ref, upd_self_ref, upd_agg_ref, upd_out_ref), slots_ref, sems)
    reads[0][2].start()
    for block in reads[1:]:
        for copy in block:
            copy.start()
    lanes = latent // LANES
    devices = far_ref.shape[0] // (2 * lanes)
    far_read.wait()
    flat_ref[...] = far_ref[...].astype(jnp.float32)
    for c in range(2):
        table_ref[pl.ds(near_total + c * devices, devices), :] = half(
            jnp.concatenate(
                [
                    flat_ref[pl.ds(c * lanes + j, devices, stride=2 * lanes), :]
                    for j in range(lanes)
                ],
                axis=1,
            )
        )
    for copy in rows:
        copy.wait()
    latent_read.wait()
    for block in reads:
        for copy in block:
            copy.wait()
    edge_out, _, upd_agg, upd_out = (weight(k)[...] for k in range(4))
    upd_self = dot(latent_ref[...], weight(1)[...])

    def gathered(block):
        span = spans[block]
        return pre_ref[span, :].astype(jnp.float32) + dot(
            picks(place_ref[span, :], table_ref.shape[0]), table_ref[...]
        )

    def settle(block, pre):
        span = spans[block]
        out = layer_norm(dot(half(silu(pre)), edge_out))
        new_ref[span, :] = half(lat_ref[span, :].astype(jnp.float32) + out)

    pre = gathered(0)
    for block in range(1, blocks):
        later = gathered(block)
        settle(block - 1, pre)
        pre = later
    settle(blocks - 1, pre)
    target = row_of(dst_ref, 0, lat_ref.shape[0] // LANES)
    inflow = half(dot(scatter_picks(target, mesh_rows), new_ref[...]))
    latent = latent_ref[...]
    act = half(silu(upd_self + dot(inflow, upd_agg)))
    out_ref[...] = half(
        latent.astype(jnp.float32) + layer_norm(dot(act, upd_out)) * gain_ref[...]
    )


def body(
    grid_input,
    grid_send,
    grid_edge_src,
    grid_edge_dst,
    edge_count,
    grid_edge_geo,
    mesh_embed,
    mesh_near_send,
    mesh_far_send,
    mesh_edge_src,
    mesh_edge_dst,
    mesh_edge_lat,
    enc_in,
    enc_out,
    send_proj,
    recv_proj,
    geo_proj,
    msg_weight,
    node_self,
    node_agg,
    node_out,
    mesh_gain,
    proc_send,
    proc_recv,
    edge_self,
    edge_out,
    upd_self,
    upd_agg,
    upd_out,
    out_gain,
):
    sub_count = lax.axis_size("sub")
    devices = lax.axis_size("band") * sub_count
    slot_cap = grid_send.shape[2]
    near_cap = mesh_near_send.shape[2]
    far_cap = mesh_far_send.shape[1]
    mesh_rows, latent = mesh_embed.shape
    edges = grid_edge_src.shape[0]
    mesh_edges = mesh_edge_src.shape[0]
    wide = 256
    bf16, f32 = jnp.bfloat16, jnp.float32

    def across_subs(parts):
        return [parts[0]] + [sub_swap(parts[k], k) for k in range(1, sub_count)]

    def across_bands(arrived):
        mates = band_swap(jnp.stack([part[1] for part in arrived]), mate)
        crosses = band_swap(jnp.stack([part[2] for part in arrived]), cross)
        return mates, crosses

    def shape(*dims, dtype=bf16):
        return jax.ShapeDtypeStruct(dims, dtype)

    received = sub_count * slot_cap
    halves = grid_input.shape[0] // 2
    parts = pl.pallas_call(
        pick_grid_kernel,
        grid=(2,),
        out_shape=(shape(3, slot_cap, wide),) * sub_count,
        in_specs=[
            pl.BlockSpec(grid_send.shape, lambda i: (0, 0, 0)),
            pl.BlockSpec((grid_input.shape[1], halves), lambda i: (0, i)),
        ],
        out_specs=(pl.BlockSpec((3, slot_cap, wide), lambda i: (0, 0, 0)),) * sub_count,
        scratch_shapes=[pltpu.VMEM((wide, 3 * received), f32)],
        compiler_params=pltpu.CompilerParams(vmem_limit_bytes=VMEM_ALL),
        cost_estimate=pl.CostEstimate(
            flops=6 * received * grid_input.shape[0] * wide,
            bytes_accessed=2 * wide * (3 * received + grid_input.shape[0]),
            transcendentals=0,
        ),
    )(grid_send, grid_input.T)
    arrived = across_subs(parts)

    far_total = devices * far_cap
    others = 3 * sub_count * near_cap + far_total
    blocks = mesh_edges // EDGE_BLOCK
    edge_src, _ = lax.optimization_barrier((grid_edge_src, parts[0]))
    edge_dst = grid_edge_dst.reshape(-1, LANES)
    mesh_src = mesh_edge_src.reshape(-1, LANES)
    mesh_dst = mesh_edge_dst.reshape(-1, LANES)
    place, own, node = local_call(
        prepare_grid_kernel,
        (
            shape(edges, LANES, dtype=f32),
            shape(edges, latent),
            shape(mesh_rows, latent, dtype=f32),
        ),
        [in_smem()] + [whole()] * 7,
        scratch=[pltpu.VMEM((384, latent), bf16)],
        flops=2 * edges * 1024 * latent,
        nbytes=16 << 20,
    )(
        edge_count,
        edge_src.reshape(-1, LANES),
        edge_dst,
        grid_edge_geo,
        mesh_embed,
        recv_proj,
        geo_proj,
        node_self,
    )

    arrived, place, own, node = lax.optimization_barrier((arrived, place, own, node))
    mates, crosses = across_bands(arrived)
    own_rows = local_call(
        encode_own_kernel,
        shape(received, latent),
        [whole()] * 7,
        flops=2 * received * 1280 * latent,
        nbytes=3 << 20,
    )(*arrived, enc_in, enc_out, send_proj)

    trio, *near_parts, far_out = local_call(
        encoder_kernel,
        (
            shape(3 * mesh_rows + 3 * near_cap, latent),
        )
        + (shape(3, near_cap, latent),) * (sub_count - 1)
        + (shape(far_total * latent // LANES, LANES),),
        [in_smem()] + [whole()] * 12 + [in_hbm()] * 7,
        scratch=[
            pltpu.VMEM((3 * received, latent), bf16),
            pltpu.VMEM((mesh_rows, latent), f32),
            pltpu.VMEM((far_total * latent // LANES, LANES), f32),
            pltpu.VMEM((PAIR, latent), bf16),
            pltpu.VMEM((7, latent, latent), bf16),
            pltpu.SemaphoreType.DMA((7,)),
        ],
        flops=2 * edges * 2048 * latent,
        nbytes=16 << 20,
    )(
        edge_count,
        own_rows,
        mates,
        crosses,
        place,
        own,
        edge_dst,
        mesh_embed,
        node,
        mesh_near_send,
        mesh_far_send.T,
        enc_in,
        mesh_gain.reshape(1, latent),
        enc_out,
        send_proj,
        msg_weight,
        node_agg,
        node_out,
        proc_send,
        proc_recv,
    )

    stay = trio[3 * mesh_rows :].reshape(3, near_cap, latent)
    near_arrived = across_subs([stay, *near_parts])
    near_arrived[1], far_out = lax.optimization_barrier((near_arrived[1], far_out))
    far_rows = lax.all_to_all(
        far_out.reshape(devices, -1, LANES),
        ("band", "sub"),
        split_axis=0,
        concat_axis=0,
        tiled=True,
    ).reshape(-1, LANES)
    near_mates, near_crosses = across_bands(near_arrived)
    pre, mesh_place = local_call(
        edge_start_kernel,
        (shape(mesh_edges, latent), shape(mesh_edges, LANES, dtype=f32)),
        [whole()] * 2 + [in_hbm()] * 3,
        scratch=[
            pltpu.VMEM((2 * mesh_rows, latent), bf16),
            pltpu.VMEM((mesh_edges, latent), bf16),
            pltpu.VMEM((latent, latent), bf16),
            pltpu.VMEM((mesh_edges, latent), bf16),
            pltpu.VMEM((mesh_edges, LANES), f32),
            pltpu.SemaphoreType.DMA((4,)),
            pltpu.SemaphoreType.DMA((3,)),
        ],
        flops=START_FLOPS,
        nbytes=START_BYTES,
        out_specs=(in_hbm(), in_hbm()),
        vmem=VMEM_ALL,
    )(mesh_src, mesh_dst, trio, mesh_edge_lat, edge_self)
    return local_call(
        edge_finish_kernel,
        shape(mesh_rows, latent),
        [whole()] * 2 + [in_hbm()] * 14,
        scratch=[
            pltpu.VMEM(far_rows.shape, bf16),
            pltpu.VMEM((mesh_rows, latent), bf16),
            pltpu.VMEM((others, latent), bf16),
            pltpu.VMEM((far_total * latent // LANES, LANES), f32),
            pltpu.VMEM((mesh_edges, latent), bf16),
            pltpu.VMEM((mesh_edges, latent), bf16),
            pltpu.VMEM((mesh_edges, LANES), f32),
            pltpu.VMEM((mesh_edges, latent), bf16),
            pltpu.VMEM((4, latent, latent), bf16),
            pltpu.SemaphoreType.DMA((6,)),
            pltpu.SemaphoreType.DMA((3 * sub_count,)),
            pltpu.SemaphoreType.DMA((3 * blocks,)),
        ],
        flops=2 * mesh_edges * 2048 * latent,
        nbytes=12 << 20,
        vmem=VMEM_ALL,
    )(
        mesh_dst,
        out_gain.reshape(1, latent),
        far_rows,
        trio,
        pre,
        mesh_place,
        mesh_edge_lat,
        *near_arrived[1:],
        near_mates,
        near_crosses,
        edge_out,
        upd_self,
        upd_agg,
        upd_out,
    )


def solution(mesh):
    rows = P(("band", "sub"), None)
    blocks = P(("band", "sub"), None, None)
    flat = P(("band", "sub"))
    return jax.shard_map(
        body,
        mesh=mesh,
        in_specs=(
            rows,
            blocks,
            flat,
            flat,
            flat,
            P(None, ("band", "sub")),
            rows,
            blocks,
            rows,
            flat,
            flat,
            rows,
        )
        + (P(),) * 18,
        out_specs=rows,
        check_vma=False,
    )
```

```python
import functools

import jax
import jax.numpy as jnp
from jax import lax
from jax.experimental import pallas as pl
from jax.experimental.pallas import tpu as pltpu
from jax.sharding import PartitionSpec as P

LANES = 128
EDGE_BLOCK = 512
PAIR = 2 * EDGE_BLOCK
VMEM_BYTES = 24 * 1024 * 1024
VMEM_ALL = 60 * 1024 * 1024
VMEM_LAST = 62650000
START_FLOPS = 4 * 10**9
START_BYTES = 16 << 20


def sub_swap(value, step):
    count = lax.axis_size("sub")
    return lax.ppermute(value, "sub", [(t, t ^ step) for t in range(count)])


def mate(band):
    return band ^ 1


def cross(band):
    return ((band + 1) ^ 1) - 1


def band_swap(value, partner):
    count = lax.axis_size("band")
    pairs = [(b, partner(b)) for b in range(count)]
    return lax.ppermute(value, "band", [(b, other) for b, other in pairs if 0 <= other < count])


def offsets():
    even = lax.rem(lax.axis_index("band"), 2) == 0
    return (1, jnp.where(even, 2, 0), jnp.where(even, 0, 2))


def sources():
    even = lax.rem(lax.axis_index("band"), 2) == 0
    return (1, jnp.where(even, 0, 2), jnp.where(even, 2, 0))


def layer_norm(values):
    row_mean = jnp.mean(values, axis=-1, keepdims=True)
    centred = values - row_mean
    variance = jnp.mean(centred * centred, axis=-1, keepdims=True)
    return centred * lax.rsqrt(variance + 1e-05)


def silu(values):
    half = 0.5 * values
    return half + half * jnp.tanh(half)


def dot(left, right):
    return jnp.dot(left, right, preferred_element_type=jnp.float32)


def half(values):
    return values.astype(jnp.bfloat16)


def column(row):
    return jnp.broadcast_to(row, (LANES, LANES)).T


def row_of(ref, first, count):
    return jnp.concatenate([ref[pl.ds(first + k, 1), :] for k in range(count)], axis=1)


def spread(rows, places):
    lanes = sum(1 for _ in places) * LANES
    lane = lax.broadcasted_iota(jnp.int32, (8, lanes), 1)
    row = lax.broadcasted_iota(jnp.int32, (8, lanes), 0)
    factors = jnp.zeros((8, lanes), jnp.float32)
    for k, entries in enumerate(places):
        for index, low, high, factor in entries:
            here = (row == index) & (lane >= k * LANES + low) & (lane < k * LANES + high)
            factors = jnp.where(here, factor, factors)
    return dot(half(rows.T), half(factors))


def digits(row):
    return [(row >> 7).astype(jnp.float32), (row & (LANES - 1)).astype(jnp.float32)]


def index_entry(first):
    return [(first, 0, LANES, float(LANES)), (first + 1, 0, LANES, 1.0)]


def lanes_of(indices):
    return lax.broadcasted_iota(jnp.int32, indices.shape, 1).astype(jnp.float32)


def picks(indices, width):
    lane = lanes_of(indices)
    indices = indices.astype(jnp.float32)
    parts = [
        half(jnp.where(indices == lane + float(first), 1.0, 0.0))
        for first in range(0, width, LANES)
    ]
    return jnp.concatenate(parts, axis=1)


def scatter_picks(row, height):
    shape = (height, row.shape[1])
    sub = lax.broadcasted_iota(jnp.int32, shape, 0)
    return half(jnp.where(sub == jnp.broadcast_to(row, shape), 1.0, 0.0))


def whole():
    return pl.BlockSpec(memory_space=pltpu.VMEM)


def in_smem():
    return pl.BlockSpec(memory_space=pltpu.SMEM)


def in_hbm():
    return pl.BlockSpec(memory_space=pltpu.HBM)


def local_call(
    kernel, out_shape, in_specs, scratch=(), flops=0, nbytes=0, out_specs=None, vmem=VMEM_BYTES
):
    return pl.pallas_call(
        kernel,
        out_shape=out_shape,
        in_specs=in_specs,
        out_specs=out_specs or jax.tree.map(lambda _: whole(), out_shape),
        scratch_shapes=list(scratch),
        compiler_params=pltpu.CompilerParams(vmem_limit_bytes=vmem),
        cost_estimate=pl.CostEstimate(flops=flops, bytes_accessed=nbytes, transcendentals=0),
    )


class Fetch:
    def __init__(self, refs, slots, sems):
        self.copies = [
            pltpu.make_async_copy(ref, slots.at[k], sems.at[k]) for k, ref in enumerate(refs)
        ]
        self.slots, self.ready = slots, set()
        for copy in self.copies:
            copy.start()

    def __call__(self, k):
        if k not in self.ready:
            self.copies[k].wait()
            self.ready.add(k)
        return self.slots.at[k]


def pick_grid_kernel(send_ref, grid_ref, *refs):
    out_refs, sum_ref = refs[:-1], refs[-1]
    width, rows = grid_ref.shape
    wide = out_refs[0].shape[-1]
    me = lax.axis_index("sub")
    part = pl.program_id(0)
    index = jnp.concatenate(
        [
            send_ref[offset, pl.ds(me ^ k, 1), :]
            for k in range(len(out_refs))
            for offset in offsets()
        ],
        axis=1,
    )
    picked = dot(grid_ref[...], scatter_picks(index - part * rows, rows))

    @pl.when(part == 0)
    def _():
        sum_ref[0:width, :] = picked
        sum_ref[width:, :] = jnp.zeros((wide - width, picked.shape[1]), jnp.float32)

    @pl.when(part > 0)
    def _():
        sum_ref[0:width, :] += picked

    @pl.when(part == pl.num_programs(0) - 1)
    def _():
        for k, out_ref in enumerate(out_refs):
            for w in range(3):
                first = (3 * k + w) * LANES
                out_ref[w] = half(sum_ref[:, first : first + LANES].T)


def prepare_grid_kernel(
    live_ref,
    src_ref,
    dst_ref,
    geo_ref,
    embed_ref,
    recv_proj_ref,
    geo_proj_ref,
    node_self_ref,
    place_ref,
    own_ref,
    node_ref,
    table_ref,
):
    mesh_rows, latent = embed_ref.shape
    base = table_ref.shape[0]
    geo_rows = geo_ref.shape[0]
    received = 3 * lax.axis_size("sub") * LANES
    is_last = lax.axis_index("band") == lax.axis_size("band") - 1
    src_shift = jnp.where(is_last, received // 3, 0)
    node_ref[...] = dot(embed_ref[...], node_self_ref[...])
    table_ref[0:mesh_rows, :] = half(dot(embed_ref[...], recv_proj_ref[...]))
    table_ref[mesh_rows:base, :] = half(
        jnp.concatenate(
            [
                geo_proj_ref[...].astype(jnp.float32),
                jnp.zeros((base - mesh_rows - geo_rows, latent), jnp.float32),
            ],
            axis=0,
        )
    )
    low = mesh_rows % LANES
    places = [
        index_entry(0),
        index_entry(2),
        [(4 + k, low + k, low + k + 1, 1.0) for k in range(geo_rows)],
    ]
    per = EDGE_BLOCK // LANES

    def step(block, carry):
        row0 = pl.multiple_of(block * EDGE_BLOCK, EDGE_BLOCK)
        rows = jnp.concatenate(
            digits(row_of(src_ref, block * per, per) - src_shift)
            + digits(row_of(dst_ref, block * per, per))
            + [geo_ref[:, pl.ds(row0, EDGE_BLOCK)].astype(jnp.float32)],
            axis=0,
        )
        wide = spread(rows, places)
        place_ref[pl.ds(row0, EDGE_BLOCK), :] = wide[:, 0:LANES]
        target = wide[:, LANES : 2 * LANES]
        lane = lanes_of(target)
        parts = []
        for k in range(base // LANES):
            part = jnp.where(target == lane + float(k * LANES), 1.0, 0.0)
            if k == mesh_rows // LANES:
                part = part + wide[:, 2 * LANES :]
            parts.append(half(part))
        own = dot(jnp.concatenate(parts, axis=1), table_ref[...])
        own_ref[pl.ds(row0, EDGE_BLOCK), :] = half(own)
        return carry

    lax.fori_loop(0, pl.cdiv(live_ref[0], PAIR) * (PAIR // EDGE_BLOCK), step, 0)


def encode_rows(rows, enc_in, enc_out, send_proj):
    hidden = half(silu(dot(rows, enc_in)))
    lat = half(layer_norm(dot(hidden, enc_out)))
    return half(dot(lat, send_proj))


def padded_rows(ref, rows):
    values = ref[...].astype(jnp.float32)
    zeros = jnp.zeros((rows - values.shape[0], values.shape[1]), jnp.float32)
    return half(jnp.concatenate([values, zeros], axis=0))


def encode_own_kernel(
    own0_ref, own1_ref, own2_ref, own3_ref, enc_in_ref, enc_out_ref, send_proj_ref, out_ref
):
    owns = (own0_ref, own1_ref, own2_ref, own3_ref)
    cap, wide = own0_ref.shape[1:]
    me = lax.axis_index("sub")
    sent = encode_rows(
        jnp.concatenate([ref[0] for ref in owns], axis=0),
        padded_rows(enc_in_ref, wide),
        enc_out_ref[...],
        send_proj_ref[...],
    )
    for k in range(len(owns)):
        out_ref[pl.ds(pl.multiple_of((me ^ k) * cap, cap), cap), :] = sent[
            k * cap : (k + 1) * cap
        ]


def encoder_kernel(
    live_ref,
    own_rows_ref,
    mate_ref,
    cross_ref,
    place_ref,
    own_ref,
    dst_ref,
    embed_ref,
    node_ref,
    near_ref,
    far_ref,
    enc_in_ref,
    gain_ref,
    enc_out_ref,
    send_proj_ref,
    msg_ref,
    node_agg_ref,
    node_out_ref,
    proc_send_ref,
    proc_recv_ref,
    trio_ref,
    out1_ref,
    out2_ref,
    out3_ref,
    out_far_ref,
    table_ref,
    sum_ref,
    flat_ref,
    act_ref,
    slots_ref,
    sems,
):
    weight = Fetch(
        (
            enc_out_ref,
            send_proj_ref,
            msg_ref,
            node_agg_ref,
            node_out_ref,
            proc_send_ref,
            proc_recv_ref,
        ),
        slots_ref,
        sems,
    )
    mesh_rows, latent = embed_ref.shape
    subs, cap, wide = mate_ref.shape
    chunk = subs * cap
    band, me = lax.axis_index("band"), lax.axis_index("sub")
    is_first = band == 0
    is_last = band == lax.axis_size("band") - 1
    polar = is_first | is_last
    live = live_ref[0]
    enc_in = padded_rows(enc_in_ref, wide)

    start = jnp.where(is_last, -chunk, 0)
    _, mate_place, cross_place = sources()
    table_ref[pl.ds(pl.multiple_of(start + chunk, chunk), chunk), :] = own_rows_ref[...]

    sent = encode_rows(
        jnp.concatenate([ref[...].reshape(chunk, wide) for ref in (mate_ref, cross_ref)], axis=0),
        enc_in,
        weight(0)[...],
        weight(1)[...],
    )
    firsts = (start + mate_place * chunk, jnp.where(polar, 2, cross_place) * chunk)
    for w, first in enumerate(firsts):
        for k in range(subs):
            place = pl.multiple_of(first + (me ^ k) * cap, cap)
            from_row = (w * subs + k) * cap
            table_ref[pl.ds(place, cap), :] = sent[from_row : from_row + cap]

    sum_ref[...] = jnp.zeros_like(sum_ref)

    def scatter(pair):
        lane = lax.broadcasted_iota(jnp.int32, (1, PAIR), 1)
        target = row_of(dst_ref, pair * (PAIR // LANES), PAIR // LANES)
        target = jnp.where(pair * PAIR + lane < live, target, -1)
        sum_ref[...] += dot(scatter_picks(target, mesh_rows), act_ref[...])

    act_ref[...] = half(
        silu(table_ref[0:PAIR, :].astype(jnp.float32) + own_ref[0:PAIR, :].astype(jnp.float32))
    )
    scatter(0)

    def edges(lookup_rows):
        def step(pair, carry):
            for k in range(PAIR // EDGE_BLOCK):
                row0 = pl.multiple_of(pair * PAIR + k * EDGE_BLOCK, EDGE_BLOCK)
                onehot = picks(place_ref[pl.ds(row0, EDGE_BLOCK), :], lookup_rows)
                pre = dot(onehot, table_ref[0:lookup_rows, :]) + own_ref[
                    pl.ds(row0, EDGE_BLOCK), :
                ].astype(jnp.float32)
                act_ref[k * EDGE_BLOCK : (k + 1) * EDGE_BLOCK, :] = half(silu(pre))
            scatter(pair)
            return carry

        lax.fori_loop(1, pl.cdiv(live, PAIR), step, 0)

    @pl.when(polar)
    def _():
        edges(2 * chunk)

    @pl.when(jnp.logical_not(polar))
    def _():
        edges(3 * chunk)

    total = sum_ref[...]
    high = half(total)
    low = half(total - high.astype(jnp.float32))
    both = dot(jnp.concatenate([high, low], axis=0), weight(2)[...])
    inflow = half(both[0:mesh_rows] + both[mesh_rows:])
    embed = embed_ref[...]
    node_act = half(silu(node_ref[...] + dot(inflow, weight(3)[...])))
    mesh_latent = half(
        embed.astype(jnp.float32) + layer_norm(dot(node_act, weight(4)[...])) * gain_ref[...]
    )
    trio_ref[2 * mesh_rows : 3 * mesh_rows, :] = mesh_latent
    sender = half(dot(mesh_latent, weight(5)[...]))
    trio_ref[0:mesh_rows, :] = sender
    trio_ref[mesh_rows : 2 * mesh_rows, :] = half(dot(mesh_latent, weight(6)[...]))
    padded = -(-mesh_rows // LANES) * LANES
    sender_pad = jnp.concatenate(
        [sender, jnp.zeros((padded - mesh_rows, latent), jnp.bfloat16)], axis=0
    )
    near = near_ref.shape[2]
    shares = offsets()
    outs = (out1_ref, out2_ref, out3_ref)
    index = jnp.concatenate(
        [near_ref[offset, pl.ds(me ^ k, 1), :] for k in range(subs) for offset in shares]
        + [far_ref[c : c + 1, :] for c in range(far_ref.shape[0])],
        axis=1,
    )
    onehot = jnp.concatenate(
        [
            picks(column(index[:, first : first + LANES]), padded)
            for first in range(0, index.shape[1], LANES)
        ],
        axis=0,
    )
    leaving = dot(onehot, sender_pad)
    trio_ref[3 * mesh_rows :, :] = half(leaving[0 : 3 * near])
    for k, out_ref in enumerate(outs, 1):
        out_ref[...] = half(leaving[3 * near * k : 3 * near * (k + 1)]).reshape(out_ref.shape)
    lanes = latent // LANES
    spread_rows = far_ref.shape[0] * lanes
    for c in range(far_ref.shape[0]):
        first = 3 * near * subs + c * LANES
        for j in range(lanes):
            flat_ref[pl.ds(c * lanes + j, LANES, stride=spread_rows), :] = leaving[
                first : first + LANES, j * LANES : (j + 1) * LANES
            ]
    out_far_ref[...] = half(flat_ref[...])


def edge_start_kernel(
    src_ref,
    dst_ref,
    trio_hbm,
    lat_hbm,
    self_hbm,
    pre_hbm,
    place_hbm,
    pair_ref,
    lat_ref,
    self_ref,
    pre_ref,
    place_ref,
    read_sems,
    write_sems,
):
    mesh_rows = pair_ref.shape[0] // 2
    subs = lax.axis_size("sub")
    devices = lax.axis_size("band") * subs
    near_total = 3 * subs * (LANES // 2)
    edges = lat_ref.shape[0]
    halves = [pl.ds(first, edges // 2) for first in (0, edges // 2)]
    pairs = pltpu.make_async_copy(
        trio_hbm.at[pl.ds(0, pair_ref.shape[0])], pair_ref, read_sems.at[3]
    )
    weight = pltpu.make_async_copy(self_hbm, self_ref, read_sems.at[2])
    reads = [
        pltpu.make_async_copy(lat_hbm.at[span], lat_ref.at[span], read_sems.at[k])
        for k, span in enumerate(halves)
    ]
    for copy in [pairs, weight, *reads]:
        copy.start()
    source = row_of(src_ref, 0, edges // LANES)
    target = row_of(dst_ref, 0, edges // LANES)
    other = source - mesh_rows
    far = other - near_total
    far = near_total + (far & 1) * devices + (far >> 1)
    rows = jnp.concatenate(
        digits(jnp.where(source < mesh_rows, source, -1))
        + digits(target + mesh_rows)
        + digits(jnp.where(other < near_total, other, far))
        + [jnp.zeros((2, edges), jnp.float32)],
        axis=0,
    )
    wide = spread(rows, [index_entry(0), index_entry(2), index_entry(4)])
    own, mine = wide[:, 0:LANES], wide[:, LANES : 2 * LANES]
    place_ref[...] = wide[:, 2 * LANES :]
    writes = [pltpu.make_async_copy(place_ref, place_hbm, write_sems.at[2])]
    writes[0].start()
    lane = lanes_of(own)
    parts = []
    for first in range(0, 2 * mesh_rows, LANES):
        hit = None
        if first < mesh_rows:
            hit = own == lane + float(first)
        if first + LANES > mesh_rows:
            match = mine == lane + float(first)
            hit = match if hit is None else hit | match
        parts.append(half(jnp.where(hit, 1.0, 0.0)))
    onehot = jnp.concatenate(parts, axis=1)
    pairs.wait()
    weight.wait()
    for k, span in enumerate(halves):
        picked = dot(onehot[k * (edges // 2) : (k + 1) * (edges // 2)], pair_ref[...])
        reads[k].wait()
        pre_ref[span, :] = half(picked + dot(lat_ref[span, :], self_ref[...]))
        writes.append(
            pltpu.make_async_copy(pre_ref.at[span], pre_hbm.at[span], write_sems.at[k])
        )
        writes[-1].start()
    for copy in writes:
        copy.wait()


def edge_finish_kernel(
    dst_ref,
    gain_ref,
    far_hbm,
    trio_hbm,
    pre_hbm,
    place_hbm,
    lat_hbm,
    own1_hbm,
    own2_hbm,
    own3_hbm,
    mate_hbm,
    cross_hbm,
    edge_out_ref,
    upd_self_ref,
    upd_agg_ref,
    upd_out_ref,
    out_ref,
    far_ref,
    latent_ref,
    table_ref,
    flat_ref,
    new_ref,
    pre_ref,
    place_ref,
    lat_ref,
    slots_ref,
    sems,
    table_sems,
    block_sems,
):
    mesh_rows, latent = latent_ref.shape
    blocks = 2
    block_rows = lat_ref.shape[0] // blocks
    spans = [pl.ds(block * block_rows, block_rows) for block in range(blocks)]
    subs, near, _ = mate_hbm.shape
    near_total = 3 * subs * near
    me = lax.axis_index("sub")
    owns = (trio_hbm, own1_hbm, own2_hbm, own3_hbm)
    stay = pl.ds(3 * latent_ref.shape[0], mate_hbm.shape[1])
    rows = []
    for w, offset in enumerate(sources()):
        for k in range(subs):
            own = owns[k].at[stay] if k == 0 else owns[k].at[0]
            source = own if w == 0 else (mate_hbm, cross_hbm)[w - 1].at[k]
            place = pl.multiple_of((offset * subs + (me ^ k)) * near, near)
            rows.append(
                pltpu.make_async_copy(
                    source, table_ref.at[pl.ds(place, near)], table_sems.at[w * subs + k]
                )
            )
    moved = ((pre_hbm, pre_ref), (place_hbm, place_ref), (lat_hbm, lat_ref))
    reads = [
        [
            pltpu.make_async_copy(hbm.at[span], ref.at[span], block_sems.at[3 * k + j])
            for j, (hbm, ref) in enumerate(moved)
        ]
        for k, span in enumerate(spans)
    ]
    far_read = pltpu.make_async_copy(far_hbm, far_ref, sems.at[4])
    latent_read = pltpu.make_async_copy(
        trio_hbm.at[pl.ds(2 * mesh_rows, mesh_rows)], latent_ref, sems.at[5]
    )
    for copy in [far_read, *rows, reads[0][1], reads[0][0], latent_read]:
        copy.start()
    weight = Fetch((edge_out_ref, upd_self_ref, upd_agg_ref, upd_out_ref), slots_ref, sems)
    reads[0][2].start()
    for block in reads[1:]:
        for copy in block:
            copy.start()
    lanes = latent // LANES
    devices = far_ref.shape[0] // (2 * lanes)
    far_read.wait()
    flat_ref[...] = far_ref[...].astype(jnp.float32)
    for c in range(2):
        table_ref[pl.ds(near_total + c * devices, devices), :] = half(
            jnp.concatenate(
                [
                    flat_ref[pl.ds(c * lanes + j, devices, stride=2 * lanes), :]
                    for j in range(lanes)
                ],
                axis=1,
            )
        )
    for copy in rows:
        copy.wait()
    latent_read.wait()
    for block in reads:
        for copy in block:
            copy.wait()
    edge_out, _, upd_agg, upd_out = (weight(k)[...] for k in range(4))
    upd_self = dot(latent_ref[...], weight(1)[...])

    def gathered(block):
        span = spans[block]
        return pre_ref[span, :].astype(jnp.float32) + dot(
            picks(place_ref[span, :], table_ref.shape[0]), table_ref[...]
        )

    def settle(block, pre):
        span = spans[block]
        out = layer_norm(dot(half(silu(pre)), edge_out))
        new_ref[span, :] = half(lat_ref[span, :].astype(jnp.float32) + out)

    pre = gathered(0)
    for block in range(1, blocks):
        later = gathered(block)
        settle(block - 1, pre)
        pre = later
    settle(blocks - 1, pre)
    target = row_of(dst_ref, 0, lat_ref.shape[0] // LANES)
    inflow = half(dot(scatter_picks(target, mesh_rows), new_ref[...]))
    latent = latent_ref[...]
    act = half(silu(upd_self + dot(inflow, upd_agg)))
    out_ref[...] = half(
        latent.astype(jnp.float32) + layer_norm(dot(act, upd_out)) * gain_ref[...]
    )


def body(
    grid_input,
    grid_send,
    grid_edge_src,
    grid_edge_dst,
    edge_count,
    grid_edge_geo,
    mesh_embed,
    mesh_near_send,
    mesh_far_send,
    mesh_edge_src,
    mesh_edge_dst,
    mesh_edge_lat,
    enc_in,
    enc_out,
    send_proj,
    recv_proj,
    geo_proj,
    msg_weight,
    node_self,
    node_agg,
    node_out,
    mesh_gain,
    proc_send,
    proc_recv,
    edge_self,
    edge_out,
    upd_self,
    upd_agg,
    upd_out,
    out_gain,
):
    sub_count = lax.axis_size("sub")
    devices = lax.axis_size("band") * sub_count
    slot_cap = grid_send.shape[2]
    near_cap = mesh_near_send.shape[2]
    far_cap = mesh_far_send.shape[1]
    mesh_rows, latent = mesh_embed.shape
    edges = grid_edge_src.shape[0]
    mesh_edges = mesh_edge_src.shape[0]
    wide = 256
    bf16, f32 = jnp.bfloat16, jnp.float32

    def across_subs(parts):
        return [parts[0]] + [sub_swap(parts[k], k) for k in range(1, sub_count)]

    def across_bands(arrived):
        mates = band_swap(jnp.stack([part[1] for part in arrived]), mate)
        crosses = band_swap(jnp.stack([part[2] for part in arrived]), cross)
        return mates, crosses

    def shape(*dims, dtype=bf16):
        return jax.ShapeDtypeStruct(dims, dtype)

    received = sub_count * slot_cap
    halves = grid_input.shape[0] // 2
    parts = pl.pallas_call(
        pick_grid_kernel,
        grid=(2,),
        out_shape=(shape(3, slot_cap, wide),) * sub_count,
        in_specs=[
            pl.BlockSpec(grid_send.shape, lambda i: (0, 0, 0)),
            pl.BlockSpec((grid_input.shape[1], halves), lambda i: (0, i)),
        ],
        out_specs=(pl.BlockSpec((3, slot_cap, wide), lambda i: (0, 0, 0)),) * sub_count,
        scratch_shapes=[pltpu.VMEM((wide, 3 * received), f32)],
        compiler_params=pltpu.CompilerParams(vmem_limit_bytes=VMEM_ALL),
        cost_estimate=pl.CostEstimate(
            flops=6 * received * grid_input.shape[0] * wide,
            bytes_accessed=2 * wide * (3 * received + grid_input.shape[0]),
            transcendentals=0,
        ),
    )(grid_send, grid_input.T)
    arrived = across_subs(parts)

    far_total = devices * far_cap
    others = 3 * sub_count * near_cap + far_total
    blocks = mesh_edges // EDGE_BLOCK
    edge_src, _ = lax.optimization_barrier((grid_edge_src, parts[0]))
    edge_dst = grid_edge_dst.reshape(-1, LANES)
    mesh_src = mesh_edge_src.reshape(-1, LANES)
    mesh_dst = mesh_edge_dst.reshape(-1, LANES)
    place, own, node = local_call(
        prepare_grid_kernel,
        (
            shape(edges, LANES, dtype=f32),
            shape(edges, latent),
            shape(mesh_rows, latent, dtype=f32),
        ),
        [in_smem()] + [whole()] * 7,
        scratch=[pltpu.VMEM((384, latent), bf16)],
        flops=2 * edges * 1024 * latent,
        nbytes=16 << 20,
    )(
        edge_count,
        edge_src.reshape(-1, LANES),
        edge_dst,
        grid_edge_geo,
        mesh_embed,
        recv_proj,
        geo_proj,
        node_self,
    )

    arrived, place, own, node = lax.optimization_barrier((arrived, place, own, node))
    mates, crosses = across_bands(arrived)
    own_rows = local_call(
        encode_own_kernel,
        shape(received, latent),
        [whole()] * 7,
        flops=2 * received * 1280 * latent,
        nbytes=3 << 20,
    )(*arrived, enc_in, enc_out, send_proj)

    trio, *near_parts, far_out = local_call(
        encoder_kernel,
        (
            shape(3 * mesh_rows + 3 * near_cap, latent),
        )
        + (shape(3, near_cap, latent),) * (sub_count - 1)
        + (shape(far_total * latent // LANES, LANES),),
        [in_smem()] + [whole()] * 12 + [in_hbm()] * 7,
        scratch=[
            pltpu.VMEM((3 * received, latent), bf16),
            pltpu.VMEM((mesh_rows, latent), f32),
            pltpu.VMEM((far_total * latent // LANES, LANES), f32),
            pltpu.VMEM((PAIR, latent), bf16),
            pltpu.VMEM((7, latent, latent), bf16),
            pltpu.SemaphoreType.DMA((7,)),
        ],
        flops=2 * edges * 2048 * latent,
        nbytes=16 << 20,
    )(
        edge_count,
        own_rows,
        mates,
        crosses,
        place,
        own,
        edge_dst,
        mesh_embed,
        node,
        mesh_near_send,
        mesh_far_send.T,
        enc_in,
        mesh_gain.reshape(1, latent),
        enc_out,
        send_proj,
        msg_weight,
        node_agg,
        node_out,
        proc_send,
        proc_recv,
    )

    stay = trio[3 * mesh_rows :].reshape(3, near_cap, latent)
    near_arrived = across_subs([stay, *near_parts])
    near_arrived[1], far_out = lax.optimization_barrier((near_arrived[1], far_out))
    far_rows = lax.all_to_all(
        far_out.reshape(devices, -1, LANES),
        ("band", "sub"),
        split_axis=0,
        concat_axis=0,
        tiled=True,
    ).reshape(-1, LANES)
    near_mates, near_crosses = across_bands(near_arrived)
    pre, mesh_place = local_call(
        edge_start_kernel,
        (shape(mesh_edges, latent), shape(mesh_edges, LANES, dtype=f32)),
        [whole()] * 2 + [in_hbm()] * 3,
        scratch=[
            pltpu.VMEM((2 * mesh_rows, latent), bf16),
            pltpu.VMEM((mesh_edges, latent), bf16),
            pltpu.VMEM((latent, latent), bf16),
            pltpu.VMEM((mesh_edges, latent), bf16),
            pltpu.VMEM((mesh_edges, LANES), f32),
            pltpu.SemaphoreType.DMA((4,)),
            pltpu.SemaphoreType.DMA((3,)),
        ],
        flops=START_FLOPS,
        nbytes=START_BYTES,
        out_specs=(in_hbm(), in_hbm()),
        vmem=VMEM_ALL,
    )(mesh_src, mesh_dst, trio, mesh_edge_lat, edge_self)
    return local_call(
        edge_finish_kernel,
        shape(mesh_rows, latent),
        [whole()] * 2 + [in_hbm()] * 14,
        scratch=[
            pltpu.VMEM(far_rows.shape, bf16),
            pltpu.VMEM((mesh_rows, latent), bf16),
            pltpu.VMEM((others, latent), bf16),
            pltpu.VMEM((far_total * latent // LANES, LANES), f32),
            pltpu.VMEM((mesh_edges, latent), bf16),
            pltpu.VMEM((mesh_edges, latent), bf16),
            pltpu.VMEM((mesh_edges, LANES), f32),
            pltpu.VMEM((mesh_edges, latent), bf16),
            pltpu.VMEM((4, latent, latent), bf16),
            pltpu.SemaphoreType.DMA((6,)),
            pltpu.SemaphoreType.DMA((3 * sub_count,)),
            pltpu.SemaphoreType.DMA((3 * blocks,)),
        ],
        flops=2 * mesh_edges * 2048 * latent,
        nbytes=12 << 20,
        vmem=VMEM_LAST,
    )(
        mesh_dst,
        out_gain.reshape(1, latent),
        far_rows,
        trio,
        pre,
        mesh_place,
        mesh_edge_lat,
        *near_arrived[1:],
        near_mates,
        near_crosses,
        edge_out,
        upd_self,
        upd_agg,
        upd_out,
    )


def solution(mesh):
    rows = P(("band", "sub"), None)
    blocks = P(("band", "sub"), None, None)
    flat = P(("band", "sub"))
    return jax.shard_map(
        body,
        mesh=mesh,
        in_specs=(
            rows,
            blocks,
            flat,
            flat,
            flat,
            P(None, ("band", "sub")),
            rows,
            blocks,
            rows,
            flat,
            flat,
            rows,
        )
        + (P(),) * 18,
        out_specs=rows,
        check_vma=False,
    )
```
